1024 devices in a mesh: group: 256 (over z, y, core), member: 4 (over x).
Axes of the slice: x: 4, y: 8, z: 16, core: 2. Of those that a mesh axis runs over, the one named last changes fastest.
Arguments:
- targets: bfloat16 [262144, 768], P(('group', 'member')), may hold values from -6 to 6
- neighbors: int32 [262144, 25], P(('group', 'member')), may hold values from 0 to 511, as said below
- hot_table: bfloat16 [2048, 768], P('member'), may hold values from -6 to 6
- hot_req: int32 [256, 4, 4, 64], P('group', 'member'), may hold values from 0 to 511
- hot_count: int32 [256, 4, 4], P('group', 'member'), may hold values from 1 to 64, as said below
- cold_table: bfloat16 [131072, 768], P('group'), may hold values from -6 to 6
- cold_owner: int32 [256, 4, 256], P('group', 'member'), may hold values from 0 to 255, as said below
- cold_row: int32 [256, 4, 256], P('group', 'member'), may hold values from 0 to 511
- w_self: bfloat16 [768, 1024], replicated, may hold values from -0.21875 to 0.21875
- w_neigh: bfloat16 [768, 1024], replicated, may hold values from -1 to 1
- bias: float32 [1024], replicated, may hold values from -3 to 3
Outputs:
- embedded: bfloat16 [262144, 1024], P(('group', 'member'))
The draws below stay inside these ranges and needn't reach their ends.
Inputs may be any that keep to these rules, and one draw needn't show every extreme that they name: `cold_owner`: each device asks exactly 2 rows of one owner group, the same group for all devices with the same member index, none of one other group and one of every remaining group. `hot_count`: in every group one member receives 64 live slots from each member of the group. `neighbors`: an entry below 256 names slot n % 64 of peer n // 64 and only live slots; others name cold request n - 256.
All inputs are finite; a program needn't handle non-finite values.
Results may differ from the reference program's by a relative error of at most 0.0039.
Values may be sent and summed in bfloat16 or wider, within the bound.
A program may use at most 128 MiB of HBM per device.

```python
import jax
import jax.numpy as jnp
from jax import lax

F = 768
HID = 1024
TGT = 256
FANOUT = 25
HCAP = 64
CCAP = 2
HOT_DEV = 512
COLD_OWN = 512
COLD_REQ = 256
TARGETS = 262144
HOT = 2048
COLD = 131072
N_GROUP = 256
N_MEMBER = 4


def live_counts(key):
    key = jax.random.fold_in(key, 101)
    first, second = jax.random.split(key)
    counts = jax.random.randint(first, (N_GROUP, N_MEMBER, N_MEMBER), 1, HCAP + 1)
    full_peer = jax.random.randint(second, (N_GROUP, 1, 1), 0, N_MEMBER)
    peers = jnp.arange(N_MEMBER, dtype=jnp.int32)[None, None, :]
    return jnp.where(peers == full_peer, HCAP, counts).astype(jnp.int32)


def draw_hot_count(key, part):
    return live_counts(key)


def draw_neighbors(key, part):
    counts = live_counts(key)
    key = jax.random.fold_in(key, 7)
    first, second, third, fourth = jax.random.split(key, 4)
    device_total = N_GROUP * N_MEMBER
    per_device = counts.reshape(device_total, N_MEMBER)
    shape = (device_total, TGT, FANOUT)
    peer = jax.random.randint(first, shape, 0, N_MEMBER)
    wide = jnp.broadcast_to(per_device[:, None, :], (device_total, TGT, N_MEMBER))
    limit = jnp.take_along_axis(wide, peer, axis=2)
    slot = jax.random.randint(second, shape, 0, limit)
    cold = jax.random.randint(third, shape, 0, COLD_REQ)
    which = jax.random.randint(fourth, shape, 0, 2)
    index = jnp.where(which == 0, peer * HCAP + slot, N_MEMBER * HCAP + cold)
    return index.reshape(device_total * TGT, FANOUT).astype(jnp.int32)


def draw_cold_owner(key, part):
    key = jax.random.fold_in(key, 3)
    first, second, third = jax.random.split(key, 3)
    device_total = N_GROUP * N_MEMBER
    busy = jax.random.randint(first, (N_MEMBER,), 0, N_GROUP)
    busy_dev = jnp.tile(busy, N_GROUP)
    scores = jax.random.randint(second, (device_total, N_GROUP - 1), 0, 2 ** 20) * N_GROUP
    scores = scores + jnp.arange(N_GROUP - 1, dtype=jnp.int32)[None, :]
    order = jnp.argsort(scores, axis=1, stable=True).astype(jnp.int32)
    others = (busy_dev[:, None] + 1 + order[:, :COLD_REQ - CCAP]) % N_GROUP
    repeated = jnp.broadcast_to(busy_dev[:, None], (device_total, CCAP))
    listed = jnp.concatenate([repeated, others], axis=1)
    mixing = jax.random.randint(third, (device_total, COLD_REQ), 0, 2 ** 20) * COLD_REQ
    mixing = mixing + jnp.arange(COLD_REQ, dtype=jnp.int32)[None, :]
    shuffle = jnp.argsort(mixing, axis=1, stable=True).astype(jnp.int32)
    listed = jnp.take_along_axis(listed, shuffle, axis=1)
    return listed.reshape(N_GROUP, N_MEMBER, COLD_REQ).astype(jnp.int32)


def touch_ends(values, own_key, smallest, high):
    longest = values.shape.index(max(values.shape))
    spots = []
    for shift in (0, 1):
        where = [jax.random.randint(jax.random.fold_in(own_key, axis), (), 0, length) for axis, length in enumerate(values.shape)]
        where[longest] = (where[longest] + shift) % values.shape[longest]
        spots.append(tuple(where))
    return values.at[spots[0]].set(smallest).at[spots[1]].set(high)


def block_scale(rng, shape, pieces, least, high):
    def one(dim, parts):
        draws = jax.random.uniform(jax.random.fold_in(jax.random.fold_in(rng, 6), dim), (parts,), jnp.float32, least / len(pieces), high / len(pieces))
        return jnp.repeat(jnp.exp(draws), shape[dim] // parts).reshape((-1,) + (1,) * (len(shape) - dim - 1))

    level = one(*pieces[0])
    for cut in pieces[1:]:
        level = level * one(*cut)
    return level


def gaussian(key, extent, spread, reach, pieces=(), held_as=jnp.bfloat16):
    loudness = block_scale(key, extent, pieces, -0.22, 0.18) if pieces else 1.0
    entries = jax.random.normal(key, extent, jnp.float32) * spread * loudness
    return jnp.minimum(jnp.maximum(entries, -reach), reach).astype(held_as)


def setup_inputs(seed: int = 0) -> dict:
    arg_keys = jax.random.split(jax.random.key(seed), 12)
    return {
        "targets": gaussian(arg_keys[0], (TARGETS, F), 1.0, 6.0, ((0, 1024),)),
        "neighbors": draw_neighbors(jax.random.fold_in(arg_keys[11], 71), 0),
        "hot_table": gaussian(arg_keys[2], (HOT, F), 1.0, 6.0, ((0, 4),)),
        "hot_req": touch_ends(jax.random.randint(arg_keys[3], (N_GROUP, N_MEMBER, N_MEMBER, HCAP), 0, HOT_DEV), jax.random.fold_in(arg_keys[3], 1), 0, HOT_DEV - 1).astype(jnp.int32),
        "hot_count": draw_hot_count(jax.random.fold_in(arg_keys[11], 71), 0),
        "cold_table": gaussian(arg_keys[5], (COLD, F), 1.0, 6.0, ((0, 256),)),
        "cold_owner": draw_cold_owner(jax.random.fold_in(arg_keys[11], 71), 0),
        "cold_row": touch_ends(jax.random.randint(arg_keys[7], (N_GROUP, N_MEMBER, COLD_REQ), 0, COLD_OWN), jax.random.fold_in(arg_keys[7], 1), 0, COLD_OWN - 1).astype(jnp.int32),
        "w_self": gaussian(arg_keys[8], (F, HID), F ** -0.5, 0.21875),
        "w_neigh": gaussian(arg_keys[9], (F, HID), (F // FANOUT) ** -0.5, 1.0),
        "bias": gaussian(arg_keys[10], (HID,), 0.5, 3.0, (), jnp.float32),
    }


def reference(targets, neighbors, hot_table, hot_req, hot_count, cold_table, cold_owner, cold_row, w_self, w_neigh, bias):
    devices_all = N_GROUP * N_MEMBER
    peers = jnp.arange(N_MEMBER, dtype=jnp.int32)
    slots = jnp.arange(HCAP, dtype=jnp.int32)

    def one_device(inputs):
        own_rows, near, asked, live, owners, wanted = inputs
        hot_index = (peers[:, None] * HOT_DEV + asked).astype(jnp.int32).reshape(-1)
        hot_rows = jnp.take(hot_table, hot_index, axis=0)
        keep = (slots[None, :] < live[:, None]).reshape(-1)
        hot_rows = jnp.where(keep[:, None], hot_rows, jnp.zeros_like(hot_rows))
        cold_index = (owners * COLD_OWN + wanted).astype(jnp.int32)
        cold_rows = jnp.take(cold_table, cold_index, axis=0)
        fetched = jnp.concatenate([hot_rows, cold_rows], axis=0)
        picked = jnp.take(fetched, near.reshape(-1).astype(jnp.int32), axis=0)
        picked = picked.reshape(TGT, FANOUT, F).astype(jnp.float32)
        aggregate = (lax.optimization_barrier(jnp.sum(picked, axis=1)) / FANOUT).astype(jnp.bfloat16)
        pre = jnp.dot(own_rows, w_self, preferred_element_type=jnp.float32)
        pre = pre + jnp.dot(aggregate, w_neigh, preferred_element_type=jnp.float32)
        pre = pre + bias.astype(jnp.float32)
        active = jnp.maximum(pre, 0.0)
        scale = lax.rsqrt(lax.optimization_barrier(jnp.mean(active * active, axis=-1, keepdims=True)) + 1e-06)
        return (active * scale).astype(jnp.bfloat16)
    result = lax.map(one_device, (targets.reshape(devices_all, TGT, F), neighbors.reshape(devices_all, TGT, FANOUT), hot_req.reshape(devices_all, N_MEMBER, HCAP), hot_count.reshape(devices_all, N_MEMBER), cold_owner.reshape(devices_all, COLD_REQ), cold_row.reshape(devices_all, COLD_REQ)))
    return result.reshape(devices_all * TGT, HID)
```

```python
import jax
import jax.numpy as jnp
from jax import lax
from jax.sharding import PartitionSpec as P

FANOUT = 25
CCAP = 2


def exchange(buffer):
    return lax.all_to_all(buffer, "group", split_axis=0, concat_axis=0, tiled=True)


def per_device(
    targets,
    neighbors,
    hot_table,
    hot_req,
    hot_count,
    cold_table,
    cold_owner,
    cold_row,
    w_self,
    w_neigh,
    bias,
):
    members = hot_req.shape[2]
    hot_slots = hot_req.shape[3]
    width = hot_table.shape[1]
    groups = lax.axis_size("group")
    asked_hot = hot_req.reshape(members, hot_slots)
    rows_out = jnp.take(
        hot_table,
        lax.all_to_all(asked_hot, "member", split_axis=0, concat_axis=0, tiled=True),
        axis=0,
    )
    hot_rows = lax.all_to_all(rows_out, "member", split_axis=0, concat_axis=0, tiled=True)
    hot_rows = hot_rows.reshape(members * hot_slots, width)
    live = hot_count.reshape(members, 1)
    keep = (jnp.arange(hot_slots, dtype=jnp.int32)[None, :] < live).reshape(-1)
    hot_rows = jnp.where(keep[:, None], hot_rows, jnp.zeros_like(hot_rows))
    owners = cold_owner.reshape(-1)
    wanted = cold_row.reshape(-1)
    requests = owners.shape[0]
    position = jnp.arange(requests, dtype=jnp.int32)
    same_owner = owners[:, None] == owners[None, :]
    earlier = position[:, None] > position[None, :]
    rank = jnp.sum((same_owner & earlier).astype(jnp.int32), axis=1)
    flat_slot = owners * CCAP + rank
    id_buffer = jnp.zeros((groups * CCAP,), jnp.int32).at[flat_slot].set(wanted)
    asked_cold = exchange(id_buffer.reshape(groups, CCAP))
    served = jnp.take(cold_table, asked_cold.reshape(-1), axis=0).reshape(groups, CCAP, width)
    returned = exchange(served)
    cold_rows = jnp.take(returned.reshape(groups * CCAP, width), flat_slot, axis=0)
    self_part = jnp.dot(targets, w_self, preferred_element_type=jnp.float32)
    fetched = jnp.concatenate([hot_rows, cold_rows], axis=0)
    columns = jnp.arange(fetched.shape[0], dtype=jnp.int32)
    tallies = jnp.sum((neighbors[:, :, None] == columns[None, None, :]).astype(jnp.float32), axis=1)
    summed = jnp.dot(tallies.astype(jnp.bfloat16), fetched, preferred_element_type=jnp.float32)
    aggregate = (summed / FANOUT).astype(jnp.bfloat16)
    pre = self_part + jnp.dot(aggregate, w_neigh, preferred_element_type=jnp.float32)
    pre = pre + bias
    active = jnp.maximum(pre, 0.0)
    scale = lax.rsqrt(jnp.mean(active * active, axis=-1, keepdims=True) + 1e-06)
    return (active * scale).astype(jnp.bfloat16)


def solution(mesh):
    return jax.shard_map(
        per_device,
        mesh=mesh,
        in_specs=(
            P(("group", "member"), None),
            P(("group", "member"), None),
            P("member", None),
            P("group", "member", None, None),
            P("group", "member", None),
            P("group", None),
            P("group", "member", None),
            P("group", "member", None),
            P(),
            P(),
            P(),
        ),
        out_specs=P(("group", "member"), None),
        check_vma=False,
    )
```

```python
import functools

import jax
import jax.numpy as jnp
from jax import lax
from jax.experimental import pallas as pl
from jax.experimental.pallas import tpu as pltpu
from jax.sharding import PartitionSpec as P

FANOUT = 25
LANES = 128
CHUNKS = 3
MESH = pl.DeviceIdType.MESH


def wait_bytes(ref, sem):
    pltpu.make_async_copy(ref, ref, sem).wait()


def one_hot(index, width):
    columns = lax.broadcasted_iota(jnp.int32, (index.shape[0], width), 1)
    return (columns == index).astype(jnp.float32).astype(jnp.bfloat16)


def lane_to_rows(row, rows, first):
    wide = jnp.broadcast_to(row, (rows, LANES))
    lane = lax.broadcasted_iota(jnp.int32, (rows, LANES), 1)
    slot = lax.broadcasted_iota(jnp.int32, (rows, LANES), 0)
    return jnp.sum(jnp.where(lane == slot + first, wide, 0), axis=1, keepdims=True)


def exact_dot(a, b):
    return jnp.dot(a, b, preferred_element_type=jnp.float32)


def exchange_kernel(
    nz,
    nyc,
    nm,
    ask_ref,
    hot_ask_ref,
    table_ref,
    hot_ref,
    cold_ref,
    extra_ref,
    hot_rows_ref,
    ids_a,
    ids_b,
    ids_c,
    hot_ids,
    square,
    hits,
    hits_x,
    z_out,
    z_in,
    y_out,
    y_in,
    x_out,
    x_in,
    row_out,
    row_in,
    h_out,
    h_in,
    send_ids,
    recv_ids,
    send_z,
    recv_z,
    send_y,
    recv_y,
    send_x,
    recv_x,
    send_h,
    recv_h,
):
    group, member = lax.axis_index("group"), lax.axis_index("member")
    z, yc = group // nyc, group % nyc
    ngroup = nz * nyc
    width = table_ref.shape[1] // CHUNKS
    owned = table_ref.shape[0]
    slots = h_out.shape[0] // nm

    def z_peer(step):
        far = nz // 2 - (step + 1) // 2
        return (z + nz + (1 - 2 * (step % 2)) * far) % nz

    def yc_peer(step):
        return (yc + 1 + step) % nyc

    def m_peer(step):
        return (member + 1 + step) % nm

    def to_z(peer):
        return (peer * nyc + yc, member)

    def to_yc(peer):
        return (z * nyc + peer, member)

    def to_m(peer):
        return (group, peer)

    def each(count, body):
        lax.fori_loop(0, count, lambda i, c: (body(i), c)[1], 0)

    def send(source, target, send_sem, recv_sem, device):
        pltpu.make_async_remote_copy(
            src_ref=source, dst_ref=target, send_sem=send_sem, recv_sem=recv_sem, device_id=device, device_id_type=MESH
        ).start()

    def block(peer, rows):
        return pl.ds(pl.multiple_of(peer * rows, rows), rows)

    barrier = pltpu.get_barrier_semaphore()

    def greet(device):
        pl.semaphore_signal(barrier, inc=1, device_id=device, device_id_type=MESH)

    each(nz - 1, lambda i: greet(to_z(z_peer(i))))
    each(nyc - 1, lambda i: greet(to_yc(yc_peer(i))))
    each(nm - 1, lambda i: greet(to_m(m_peer(i))))
    pl.semaphore_wait(barrier, nz + nyc + nm - 3)

    def send_ids_yc(i):
        peer = yc_peer(i)
        send(ask_ref.at[peer], ids_a.at[yc], send_ids.at[0], recv_ids.at[0], to_yc(peer))

    each(nyc - 1, send_ids_yc)

    def send_ids_m(i):
        peer = m_peer(i)
        send(hot_ask_ref.at[peer], hot_ids.at[member], send_ids.at[2], recv_ids.at[2], to_m(peer))

    each(nm - 1, send_ids_m)
    ids_a[yc] = ask_ref[yc]
    hot_ids[member] = hot_ask_ref[member]
    square[...] = jnp.zeros_like(square)

    wait_bytes(ids_a.at[pl.ds(0, nyc - 1)], recv_ids.at[0])
    for peer in range(nyc):
        square[peer : peer + 1, :] = ids_a[peer, 0:1, :]
        square[nyc + peer : nyc + peer + 1, :] = ids_a[peer, 1:2, :]
    square[...] = square[...].T
    for peer in range(nz):
        ids_b[peer] = square[peer : peer + 1, :]

    def send_ids_z(i):
        peer = z_peer(i)
        send(ids_b.at[peer], ids_c.at[z], send_ids.at[1], recv_ids.at[1], to_z(peer))

    each(nz - 1, send_ids_z)
    ids_c[z] = ids_b[z]

    wait_bytes(hot_ids.at[pl.ds(0, nm - 1)], recv_ids.at[2])
    for peer in range(nm):
        wanted = one_hot(lane_to_rows(hot_ids[peer], slots, 0), hot_ref.shape[0])
        h_out[peer * slots : (peer + 1) * slots, :] = exact_dot(wanted, hot_ref[...]).astype(jnp.bfloat16)

    def send_hot(i):
        peer = m_peer(i)
        send(h_out.at[block(peer, slots)], h_in.at[block(member, slots)], send_h, recv_h, to_m(peer))

    each(nm - 1, send_hot)
    h_in[block(member, slots), :] = h_out[block(member, slots), :]

    rows_to = lax.broadcasted_iota(jnp.int32, (ngroup, ngroup), 0)
    rows_from = lax.broadcasted_iota(jnp.int32, (ngroup, ngroup), 1)
    turn = (rows_from == lax.rem(rows_to, nz) * nyc + lax.div(rows_to, nz)).astype(jnp.float32).astype(jnp.bfloat16)

    wait_bytes(ids_c.at[pl.ds(0, nz - 1)], recv_ids.at[1])
    for peer in range(nz):
        hits[peer * nyc : (peer + 1) * nyc, :] = one_hot(lane_to_rows(ids_c[peer], nyc, 0), owned)
        hits_x[peer * nyc : (peer + 1) * nyc, :] = one_hot(lane_to_rows(ids_c[peer], nyc, nyc), owned)

    def gather_and_send(chunk):
        z_out[chunk] = exact_dot(hits[...], table_ref[:, chunk * width : (chunk + 1) * width]).astype(jnp.bfloat16)

        def send_rows(i):
            peer = z_peer(i)
            send(
                z_out.at[chunk, block(peer, nyc)],
                z_in.at[chunk, block(z, nyc)],
                send_z.at[chunk],
                recv_z.at[chunk],
                to_z(peer),
            )

        each(nz - 1, send_rows)
        z_in[chunk, block(z, nyc), :] = z_out[chunk, block(z, nyc), :]

    gather_and_send(0)

    ordered = exact_dot(turn, hits_x[...]).astype(jnp.bfloat16)
    x_out[...] = exact_dot(ordered, table_ref[...]).astype(jnp.bfloat16)

    def send_extra(i):
        peer = yc_peer(i)
        send(x_out.at[block(peer, nz)], x_in.at[block(yc, nz)], send_x.at[0], recv_x.at[0], to_yc(peer))

    each(nyc - 1, send_extra)
    x_in[block(yc, nz), :] = x_out[block(yc, nz), :]

    for chunk in range(1, CHUNKS):
        gather_and_send(chunk)

    def turn_and_send(chunk):
        wait_bytes(z_in.at[chunk, pl.ds(0, (nz - 1) * nyc)], recv_z.at[chunk])
        y_out[chunk] = exact_dot(turn, z_in[chunk]).astype(jnp.bfloat16)

        def send_rows(i):
            peer = yc_peer(i)
            send(
                y_out.at[chunk, block(peer, nz)],
                y_in.at[chunk, block(yc, nz)],
                send_y.at[chunk],
                recv_y.at[chunk],
                to_yc(peer),
            )

        each(nyc - 1, send_rows)
        y_in[chunk, block(yc, nz), :] = y_out[chunk, block(yc, nz), :]

    turn_and_send(0)

    wait_bytes(x_in.at[pl.ds(0, (nyc - 1) * nz)], recv_x.at[0])
    target = lax.broadcasted_iota(jnp.int32, (nz, ngroup), 0)
    source = lax.broadcasted_iota(jnp.int32, (nz, ngroup), 1)
    pick = (lax.rem(source, nz) == target).astype(jnp.float32).astype(jnp.bfloat16)
    picked = exact_dot(pick, x_in[...])
    for peer in range(nz):
        row_out[peer] = picked[peer : peer + 1, :]

    def send_extra_row(i):
        peer = z_peer(i)
        send(row_out.at[peer], row_in.at[z], send_x.at[1], recv_x.at[1], to_z(peer))

    each(nz - 1, send_extra_row)
    row_in[z] = row_out[z]

    for chunk in range(1, CHUNKS):
        turn_and_send(chunk)

    wait_bytes(h_in.at[pl.ds(0, (nm - 1) * slots)], recv_h)
    hot_rows_ref[...] = h_in[...]
    wait_bytes(row_in.at[pl.ds(0, nz - 1)], recv_x.at[1])
    extra = row_in[0]
    for peer in range(1, nz):
        extra = extra + row_in[peer]
    extra_ref[...] = extra
    for chunk in range(CHUNKS):
        wait_bytes(y_in.at[chunk, pl.ds(0, (nyc - 1) * nz)], recv_y.at[chunk])
        cold_ref[:, chunk * width : (chunk + 1) * width] = y_in[chunk]

    wait_bytes(ids_a.at[pl.ds(0, nyc - 1)], send_ids.at[0])
    wait_bytes(ids_c.at[pl.ds(0, nz - 1)], send_ids.at[1])
    wait_bytes(hot_ids.at[pl.ds(0, nm - 1)], send_ids.at[2])
    wait_bytes(h_in.at[pl.ds(0, (nm - 1) * slots)], send_h)
    wait_bytes(x_in.at[pl.ds(0, (nyc - 1) * nz)], send_x.at[0])
    wait_bytes(row_in.at[pl.ds(0, nz - 1)], send_x.at[1])
    for chunk in range(CHUNKS):
        wait_bytes(z_in.at[chunk, pl.ds(0, (nz - 1) * nyc)], send_z.at[chunk])
        wait_bytes(y_in.at[chunk, pl.ds(0, (nyc - 1) * nz)], send_y.at[chunk])


def exchange(nz, nyc, nm, ask, hot_ask, cold_table, hot_table):
    ngroup = nz * nyc
    owned, features = cold_table.shape
    slots = hot_ask.shape[-1]
    hot_ask = jnp.pad(hot_ask, ((0, 0), (0, LANES - slots))).reshape(nm, 1, LANES)
    bf16, f32, i32 = jnp.bfloat16, jnp.float32, jnp.int32
    vmem = pl.BlockSpec(memory_space=pltpu.VMEM)
    chunked = pltpu.VMEM((CHUNKS, ngroup, features // CHUNKS), bf16)
    dma = pltpu.SemaphoreType.DMA
    return pl.pallas_call(
        functools.partial(exchange_kernel, nz, nyc, nm),
        out_shape=(
            jax.ShapeDtypeStruct((ngroup, features), bf16),
            jax.ShapeDtypeStruct((1, features), f32),
            jax.ShapeDtypeStruct((nm * slots, features), bf16),
        ),
        in_specs=[vmem] * 4,
        out_specs=(vmem,) * 3,
        scratch_shapes=[
            pltpu.VMEM((nyc, 2, LANES), i32),
            pltpu.VMEM((nz, 1, LANES), i32),
            pltpu.VMEM((nz, 1, LANES), i32),
            pltpu.VMEM((nm, 1, LANES), i32),
            pltpu.VMEM((LANES, LANES), i32),
            pltpu.VMEM((ngroup, owned), bf16),
            pltpu.VMEM((ngroup, owned), bf16),
            chunked,
            chunked,
            chunked,
            chunked,
            pltpu.VMEM((ngroup, features), bf16),
            pltpu.VMEM((ngroup, features), bf16),
            pltpu.VMEM((nz, 1, features), f32),
            pltpu.VMEM((nz, 1, features), f32),
            pltpu.VMEM((nm * slots, features), bf16),
            pltpu.VMEM((nm * slots, features), bf16),
            dma((3,)),
            dma((3,)),
            dma((CHUNKS,)),
            dma((CHUNKS,)),
            dma((CHUNKS,)),
            dma((CHUNKS,)),
            dma((2,)),
            dma((2,)),
            dma,
            dma,
        ],
        compiler_params=pltpu.CompilerParams(
            collective_id=0, has_side_effects=True, vmem_limit_bytes=32 * 1024 * 1024
        ),
    )(ask, hot_ask, cold_table, hot_table)


def per_device(
    nz,
    nyc,
    targets,
    neighbors,
    hot_table,
    hot_req,
    hot_count,
    cold_table,
    cold_owner,
    cold_row,
    w_self,
    w_neigh,
    bias,
):
    members, hot_slots = hot_req.shape[2:]
    groups = nz * nyc
    owners, wanted = cold_owner.reshape(-1), cold_row.reshape(-1)
    requests = owners.shape[0]
    owned = cold_table.shape[0]

    position = jnp.arange(requests, dtype=jnp.int32)
    coded = (position * owned + wanted)[:, None]
    asked = owners[:, None] == jnp.arange(groups, dtype=jnp.int32)[None, :]
    first = jnp.min(jnp.where(asked, coded, requests * owned), axis=0)
    last = jnp.max(jnp.where(asked, coded, -1), axis=0)
    twice = last > first
    first_row = jnp.where(first < requests * owned, first % owned, 0)
    last_row = jnp.where(twice, last % owned, -1)
    ask = jnp.stack([first_row.reshape(nz, nyc).T, last_row.reshape(nz, nyc).T], axis=1)
    ask = jnp.pad(ask, ((0, 0), (0, 0), (0, LANES - nz)))

    cold, extra, hot = exchange(
        nz, nyc, members, ask, hot_req.reshape(members, hot_slots), cold_table, hot_table
    )

    self_part = jnp.dot(targets, w_self, preferred_element_type=jnp.float32)
    columns = jnp.arange(members * hot_slots + requests, dtype=jnp.int32)
    tallies = jnp.sum((neighbors[:, :, None] == columns[None, None, :]).astype(jnp.float32), axis=1)
    keep = (jnp.arange(hot_slots, dtype=jnp.int32)[None, :] < hot_count.reshape(members, 1)).reshape(-1)
    hot_tally = jnp.where(keep[None, :], tallies[:, : members * hot_slots], 0.0).astype(jnp.bfloat16)
    cold_tally = tallies[:, members * hot_slots :].astype(jnp.bfloat16)
    first_at = jnp.where(first < requests * owned, first // owned, -1).reshape(nz, nyc).T.reshape(-1)
    last_at = jnp.max(jnp.where(twice, last // owned, -1))
    place = (position[:, None] == first_at[None, :]).astype(jnp.bfloat16)
    placed = jnp.dot(cold_tally, place, preferred_element_type=jnp.float32).astype(jnp.bfloat16)
    second = jnp.sum(jnp.where(position[None, :] == last_at, tallies[:, members * hot_slots :], 0.0), axis=1)
    summed = jnp.dot(hot_tally, hot, preferred_element_type=jnp.float32)
    summed = summed + jnp.dot(placed, cold, preferred_element_type=jnp.float32)
    summed = summed + second[:, None] * extra
    aggregate = (summed / FANOUT).astype(jnp.bfloat16)
    pre = self_part + jnp.dot(aggregate, w_neigh, preferred_element_type=jnp.float32)
    pre = pre + bias
    active = jnp.maximum(pre, 0.0)
    scale = lax.rsqrt(jnp.mean(active * active, axis=-1, keepdims=True) + 1e-06)
    return (active * scale).astype(jnp.bfloat16)


def solution(mesh, nyc=16):
    nz = mesh.shape["group"] // nyc
    return jax.shard_map(
        functools.partial(per_device, nz, nyc),
        mesh=mesh,
        in_specs=(
            P(("group", "member"), None),
            P(("group", "member"), None),
            P("member", None),
            P("group", "member", None, None),
            P("group", "member", None),
            P("group", None),
            P("group", "member", None),
            P("group", "member", None),
            P(),
            P(),
            P(),
        ),
        out_specs=P(("group", "member"), None),
        check_vma=False,
    )
```

```python
import functools

import jax
import jax.numpy as jnp
from jax import lax
from jax.experimental import pallas as pl
from jax.experimental.pallas import tpu as pltpu
from jax.sharding import PartitionSpec as P

FANOUT = 25
LANES = 128
CHUNKS = 3
MESH = pl.DeviceIdType.MESH


def wait_bytes(ref, sem):
    pltpu.make_async_copy(ref, ref, sem).wait()


def one_hot(index, width):
    columns = lax.broadcasted_iota(jnp.int32, (index.shape[0], width), 1)
    return (columns == index).astype(jnp.float32).astype(jnp.bfloat16)


def lane_to_rows(row, rows, first):
    wide = jnp.broadcast_to(row, (rows, LANES))
    lane = lax.broadcasted_iota(jnp.int32, (rows, LANES), 1)
    slot = lax.broadcasted_iota(jnp.int32, (rows, LANES), 0)
    return jnp.sum(jnp.where(lane == slot + first, wide, 0), axis=1, keepdims=True)


def exact_dot(a, b):
    return jnp.dot(a, b, preferred_element_type=jnp.float32)


def layer_kernel(
    nz,
    nyc,
    nm,
    targets_hbm,
    near_hbm,
    hot_hbm,
    hot_req_hbm,
    live_hbm,
    table_hbm,
    owner_hbm,
    wanted_hbm,
    w_self_hbm,
    w_neigh_hbm,
    bias_hbm,
    out_ref,
    targets_ref,
    near_ref,
    hot_ref,
    hot_req_ref,
    live_ref,
    table_ref,
    owner_ref,
    wanted_ref,
    w_self_ref,
    w_neigh_ref,
    bias_ref,
    ask,
    hot_ask,
    ids_a,
    ids_b,
    ids_c,
    hot_ids,
    square,
    hits,
    hits_x,
    z_out,
    z_in,
    y_out,
    y_in,
    x_out,
    x_in,
    row_out,
    row_in,
    h_out,
    h_in,
    tally,
    summed,
    total,
    load_sem,
    send_ids,
    recv_ids,
    send_z,
    recv_z,
    send_y,
    recv_y,
    send_x,
    recv_x,
    send_h,
    recv_h,
):
    group, member = lax.axis_index("group"), lax.axis_index("member")
    z, yc = group // nyc, group % nyc
    ngroup = nz * nyc
    owned, features = table_ref.shape
    width = features // CHUNKS
    slots = h_out.shape[0] // nm
    hot_slots = nm * slots
    rows = targets_ref.shape[0]
    bf16, f32, i32 = jnp.bfloat16, jnp.float32, jnp.int32

    def iota(shape, dim):
        return lax.broadcasted_iota(i32, shape, dim)

    def z_peer(step):
        far = nz // 2 - (step + 1) // 2
        return (z + nz + (1 - 2 * (step % 2)) * far) % nz

    def yc_peer(step):
        return (yc + 1 + step) % nyc

    def m_peer(step):
        return (member + 1 + step) % nm

    def to_z(peer):
        return (peer * nyc + yc, member)

    def to_yc(peer):
        return (z * nyc + peer, member)

    def to_m(peer):
        return (group, peer)

    def each(count, body):
        lax.fori_loop(0, count, lambda i, c: (body(i), c)[1], 0)

    def send(source, target, send_sem, recv_sem, device):
        pltpu.make_async_remote_copy(
            src_ref=source, dst_ref=target, send_sem=send_sem, recv_sem=recv_sem, device_id=device, device_id_type=MESH
        ).start()

    def block(peer, count):
        return pl.ds(pl.multiple_of(peer * count, count), count)

    loads = [
        pltpu.make_async_copy(source, target, load_sem.at[number])
        for number, (source, target) in enumerate(
            [
                (owner_hbm, owner_ref),
                (wanted_hbm, wanted_ref),
                (hot_req_hbm, hot_req_ref),
                (live_hbm, live_ref),
                (bias_hbm, bias_ref),
                (hot_hbm, hot_ref),
                (table_hbm, table_ref),
                (near_hbm, near_ref),
                (targets_hbm, targets_ref),
                (w_self_hbm, w_self_ref),
                (w_neigh_hbm, w_neigh_ref),
            ]
        )
    ]
    for load in loads:
        load.start()

    barrier = pltpu.get_barrier_semaphore()

    def greet(device):
        pl.semaphore_signal(barrier, inc=1, device_id=device, device_id_type=MESH)

    each(nyc - 1, lambda i: greet(to_yc(yc_peer(i))))
    each(nz - 1, lambda i: greet(to_z(z_peer(i))))
    each(nm - 1, lambda i: greet(to_m(m_peer(i))))

    for load in loads[:3]:
        load.wait()
    requests = owner_ref.shape[-1]
    owners = owner_ref[0]
    coded = iota((1, requests), 1) * owned + wanted_ref[0]
    asked = jnp.broadcast_to(owners, (ngroup, requests)) == iota((ngroup, requests), 0)
    coded = jnp.broadcast_to(coded, (ngroup, requests))
    first = jnp.min(jnp.where(asked, coded, requests * owned), axis=1, keepdims=True)
    last = jnp.max(jnp.where(asked, coded, -1), axis=1, keepdims=True)
    twice = last > first
    first_row = jnp.where(first < requests * owned, lax.rem(first, owned), 0)
    last_row = jnp.where(twice, lax.rem(last, owned), -1)
    lane = iota((nyc, LANES), 1)
    packed = jnp.zeros((nyc, LANES), i32)
    for peer in range(nz):
        part = slice(peer * nyc, (peer + 1) * nyc)
        packed = jnp.where(lane == peer, first_row[part], packed)
        packed = jnp.where(lane == nz + peer, last_row[part], packed)
    for peer in range(nyc):
        ask[peer] = packed[peer : peer + 1]
    for peer in range(nm):
        hot_ask[peer] = jnp.zeros((1, LANES), i32)
        hot_ask[peer, :, 0:slots] = hot_req_ref[0, 0, peer : peer + 1, :]

    pl.semaphore_wait(barrier, nz + nyc + nm - 3)

    def send_ids_yc(i):
        peer = yc_peer(i)
        send(ask.at[peer], ids_a.at[yc], send_ids.at[0], recv_ids.at[0], to_yc(peer))

    each(nyc - 1, send_ids_yc)

    def send_ids_m(i):
        peer = m_peer(i)
        send(hot_ask.at[peer], hot_ids.at[member], send_ids.at[2], recv_ids.at[2], to_m(peer))

    each(nm - 1, send_ids_m)
    ids_a[yc] = ask[yc]
    hot_ids[member] = hot_ask[member]
    square[...] = jnp.zeros_like(square)

    wait_bytes(ids_a.at[pl.ds(0, nyc - 1)], recv_ids.at[0])
    for peer in range(nyc):
        square[peer : peer + 1, :] = ids_a[peer]
    square[...] = square[...].T
    for peer in range(nz):
        ids_b[peer, :, 0:nyc] = square[peer : peer + 1, 0:nyc]
        ids_b[peer, :, nyc : 2 * nyc] = square[nz + peer : nz + peer + 1, 0:nyc]

    def send_ids_z(i):
        peer = z_peer(i)
        send(ids_b.at[peer], ids_c.at[z], send_ids.at[1], recv_ids.at[1], to_z(peer))

    each(nz - 1, send_ids_z)
    ids_c[z] = ids_b[z]

    wait_bytes(hot_ids.at[pl.ds(0, nm - 1)], recv_ids.at[2])
    loads[5].wait()
    for peer in range(nm):
        wanted_rows = one_hot(lane_to_rows(hot_ids[peer], slots, 0), hot_ref.shape[0])
        h_out[peer * slots : (peer + 1) * slots, :] = exact_dot(wanted_rows, hot_ref[...]).astype(bf16)

    def send_hot(i):
        peer = m_peer(i)
        send(h_out.at[block(peer, slots)], h_in.at[block(member, slots)], send_h, recv_h, to_m(peer))

    each(nm - 1, send_hot)
    h_in[block(member, slots), :] = h_out[block(member, slots), :]

    rows_to = iota((ngroup, ngroup), 0)
    rows_from = iota((ngroup, ngroup), 1)
    turn = (rows_from == lax.rem(rows_to, nz) * nyc + lax.div(rows_to, nz)).astype(f32).astype(bf16)

    loads[6].wait()
    wait_bytes(ids_c.at[pl.ds(0, nz - 1)], recv_ids.at[1])
    for peer in range(nz):
        hits[peer * nyc : (peer + 1) * nyc, :] = one_hot(lane_to_rows(ids_c[peer], nyc, 0), owned)

    def gather_and_send(chunk):
        z_out[chunk] = exact_dot(hits[...], table_ref[:, chunk * width : (chunk + 1) * width]).astype(bf16)

        def send_rows(i):
            peer = z_peer(i)
            send(
                z_out.at[chunk, block(peer, nyc)],
                z_in.at[chunk, block(z, nyc)],
                send_z.at[chunk],
                recv_z.at[chunk],
                to_z(peer),
            )

        each(nz - 1, send_rows)
        z_in[chunk, block(z, nyc), :] = z_out[chunk, block(z, nyc), :]

    gather_and_send(0)

    for peer in range(nz):
        hits_x[peer * nyc : (peer + 1) * nyc, :] = one_hot(lane_to_rows(ids_c[peer], nyc, nyc), owned)
    ordered = exact_dot(turn, hits_x[...]).astype(bf16)
    x_out[...] = exact_dot(ordered, table_ref[...]).astype(bf16)

    def send_extra(i):
        peer = yc_peer(i)
        send(x_out.at[block(peer, nz)], x_in.at[block(yc, nz)], send_x.at[0], recv_x.at[0], to_yc(peer))

    each(nyc - 1, send_extra)
    x_in[block(yc, nz), :] = x_out[block(yc, nz), :]

    for chunk in range(1, CHUNKS):
        gather_and_send(chunk)

    def turn_and_send(chunk):
        wait_bytes(z_in.at[chunk, pl.ds(0, (nz - 1) * nyc)], recv_z.at[chunk])
        y_out[chunk] = exact_dot(turn, z_in[chunk]).astype(bf16)

        def send_rows(i):
            peer = yc_peer(i)
            send(
                y_out.at[chunk, block(peer, nz)],
                y_in.at[chunk, block(yc, nz)],
                send_y.at[chunk],
                recv_y.at[chunk],
                to_yc(peer),
            )

        each(nyc - 1, send_rows)
        y_in[chunk, block(yc, nz), :] = y_out[chunk, block(yc, nz), :]

    loads[7].wait()
    loads[3].wait()
    near = near_ref[...]
    for first_column in range(0, tally.shape[1], LANES):
        span = min(LANES, tally.shape[1] - first_column)
        columns = iota((rows, span), 1) + first_column
        counted = jnp.zeros((rows, span), f32)
        for j in range(near.shape[1]):
            counted = counted + jnp.where(near[:, j : j + 1] == columns, 1.0, 0.0)
        tally[:, first_column : first_column + span] = counted
    slot = iota((1, hot_slots), 1)
    limit = jnp.zeros((1, hot_slots), i32)
    for peer in range(nm):
        limit = jnp.where(lax.div(slot, slots) == peer, live_ref[0, :, peer : peer + 1], limit)
    hot_tally = jnp.where(lax.rem(slot, slots) < limit, tally[:, 0:hot_slots], 0.0).astype(bf16)
    cold_tally = tally[:, hot_slots:]
    position = iota((ngroup, requests), 1)
    place = (position == lax.div(first, owned)).astype(f32).astype(bf16)
    place = exact_dot(turn, place).astype(bf16)
    placed = lax.dot_general(
        cold_tally.astype(bf16), place, (((1,), (1,)), ((), ())), preferred_element_type=f32
    ).astype(bf16)
    last_at = jnp.max(jnp.where(twice, lax.div(last, owned), -1), axis=0, keepdims=True)
    second = jnp.sum(jnp.where(iota((1, requests), 1) == last_at, cold_tally, 0.0), axis=1, keepdims=True)

    for load in loads[8:10]:
        load.wait()
    loads[4].wait()
    total[...] = exact_dot(targets_ref[...], w_self_ref[...]) + bias_ref[...].reshape(1, -1)

    turn_and_send(0)

    wait_bytes(x_in.at[pl.ds(0, (nyc - 1) * nz)], recv_x.at[0])
    target = iota((nz, ngroup), 0)
    source = iota((nz, ngroup), 1)
    pick = (lax.rem(source, nz) == target).astype(f32).astype(bf16)
    picked = exact_dot(pick, x_in[...])
    for peer in range(nz):
        row_out[peer] = picked[peer : peer + 1, :]

    def send_extra_row(i):
        peer = z_peer(i)
        send(row_out.at[peer], row_in.at[z], send_x.at[1], recv_x.at[1], to_z(peer))

    each(nz - 1, send_extra_row)
    row_in[z] = row_out[z]

    wait_bytes(h_in.at[pl.ds(0, (nm - 1) * slots)], recv_h)
    summed[...] = exact_dot(hot_tally, h_in[...])

    for chunk in range(1, CHUNKS):
        turn_and_send(chunk)

    wait_bytes(row_in.at[pl.ds(0, nz - 1)], recv_x.at[1])
    extra = row_in[0]
    for peer in range(1, nz):
        extra = extra + row_in[peer]
    summed[...] = summed[...] + second * extra
    loads[10].wait()
    for chunk in range(CHUNKS):
        part = slice(chunk * width, (chunk + 1) * width)
        wait_bytes(y_in.at[chunk, pl.ds(0, (nyc - 1) * nz)], recv_y.at[chunk])
        aggregate = summed[:, part] + exact_dot(placed, y_in[chunk])
        aggregate = (aggregate * (1.0 / FANOUT)).astype(bf16)
        total[...] = total[...] + exact_dot(aggregate, w_neigh_ref[part, :])
    active = jnp.maximum(total[...], 0.0)
    scale = lax.rsqrt(jnp.mean(active * active, axis=-1, keepdims=True) + 1e-06)
    out_ref[...] = (active * scale).astype(bf16)

    wait_bytes(ids_a.at[pl.ds(0, nyc - 1)], send_ids.at[0])
    wait_bytes(ids_c.at[pl.ds(0, nz - 1)], send_ids.at[1])
    wait_bytes(hot_ids.at[pl.ds(0, nm - 1)], send_ids.at[2])
    wait_bytes(h_in.at[pl.ds(0, (nm - 1) * slots)], send_h)
    wait_bytes(x_in.at[pl.ds(0, (nyc - 1) * nz)], send_x.at[0])
    wait_bytes(row_in.at[pl.ds(0, nz - 1)], send_x.at[1])
    for chunk in range(CHUNKS):
        wait_bytes(z_in.at[chunk, pl.ds(0, (nz - 1) * nyc)], send_z.at[chunk])
        wait_bytes(y_in.at[chunk, pl.ds(0, (nyc - 1) * nz)], send_y.at[chunk])


def per_device(nz, nyc, *args):
    targets, near, hot_table, hot_req, live, cold_table, owner, wanted, w_self, w_neigh, bias = args
    nm, slots = hot_req.shape[2:]
    ngroup = nz * nyc
    owned, features = cold_table.shape
    rows, hidden = targets.shape[0], w_self.shape[1]
    bf16, f32, i32 = jnp.bfloat16, jnp.float32, jnp.int32
    chunked = pltpu.VMEM((CHUNKS, ngroup, features // CHUNKS), bf16)
    dma = pltpu.SemaphoreType.DMA
    return pl.pallas_call(
        functools.partial(layer_kernel, nz, nyc, nm),
        out_shape=jax.ShapeDtypeStruct((rows, hidden), bf16),
        in_specs=[pl.BlockSpec(memory_space=pl.ANY)] * len(args),
        out_specs=pl.BlockSpec(memory_space=pltpu.VMEM),
        scratch_shapes=[pltpu.VMEM(a.shape, a.dtype) for a in args]
        + [
            pltpu.VMEM((nyc, 1, LANES), i32),
            pltpu.VMEM((nm, 1, LANES), i32),
            pltpu.VMEM((nyc, 1, LANES), i32),
            pltpu.VMEM((nz, 1, LANES), i32),
            pltpu.VMEM((nz, 1, LANES), i32),
            pltpu.VMEM((nm, 1, LANES), i32),
            pltpu.VMEM((LANES, LANES), i32),
            pltpu.VMEM((ngroup, owned), bf16),
            pltpu.VMEM((ngroup, owned), bf16),
            chunked,
            chunked,
            chunked,
            chunked,
            pltpu.VMEM((ngroup, features), bf16),
            pltpu.VMEM((ngroup, features), bf16),
            pltpu.VMEM((nz, 1, features), f32),
            pltpu.VMEM((nz, 1, features), f32),
            pltpu.VMEM((nm * slots, features), bf16),
            pltpu.VMEM((nm * slots, features), bf16),
            pltpu.VMEM((rows, nm * slots + owner.shape[-1]), f32),
            pltpu.VMEM((rows, features), f32),
            pltpu.VMEM((rows, hidden), f32),
            dma((len(args),)),
            dma((3,)),
            dma((3,)),
            dma((CHUNKS,)),
            dma((CHUNKS,)),
            dma((CHUNKS,)),
            dma((CHUNKS,)),
            dma((2,)),
            dma((2,)),
            dma,
            dma,
        ],
        compiler_params=pltpu.CompilerParams(
            collective_id=0, has_side_effects=True, vmem_limit_bytes=48 * 1024 * 1024
        ),
        cost_estimate=pl.CostEstimate(
            flops=4 * rows * features * hidden, bytes_accessed=8 * 1024 * 1024, transcendentals=rows
        ),
    )(*args)


def solution(mesh, nyc=16):
    nz = mesh.shape["group"] // nyc
    return jax.shard_map(
        functools.partial(per_device, nz, nyc),
        mesh=mesh,
        in_specs=(
            P(("group", "member"), None),
            P(("group", "member"), None),
            P("member", None),
            P("group", "member", None, None),
            P("group", "member", None),
            P("group", None),
            P("group", "member", None),
            P("group", "member", None),
            P(),
            P(),
            P(),
        ),
        out_specs=P(("group", "member"), None),
        check_vma=False,
    )
```

```python
import functools

import jax
import jax.numpy as jnp
from jax import lax
from jax.experimental import pallas as pl
from jax.experimental.pallas import tpu as pltpu
from jax.sharding import PartitionSpec as P

FANOUT = 25
LANES = 128
CHUNKS = 3
MESH = pl.DeviceIdType.MESH


def wait_bytes(ref, sem):
    pltpu.make_async_copy(ref, ref, sem).wait()


def one_hot(index, width):
    columns = lax.broadcasted_iota(jnp.int32, (index.shape[0], width), 1)
    return (columns == index).astype(jnp.float32).astype(jnp.bfloat16)


def lane_to_rows(row, rows, first):
    wide = jnp.broadcast_to(row, (rows, LANES))
    lane = lax.broadcasted_iota(jnp.int32, (rows, LANES), 1)
    slot = lax.broadcasted_iota(jnp.int32, (rows, LANES), 0)
    return jnp.sum(jnp.where(lane == slot + first, wide, 0), axis=1, keepdims=True)


def exact_dot(a, b):
    return jnp.dot(a, b, preferred_element_type=jnp.float32)


def count_dot(counts, values):
    return lax.dot_general(counts, values, (((0,), (0,)), ((), ())), preferred_element_type=jnp.float32)


def layer_kernel(
    nz,
    nyc,
    nm,
    targets_hbm,
    near_hbm,
    hot_hbm,
    hot_req_hbm,
    live_hbm,
    table_hbm,
    owner_hbm,
    wanted_hbm,
    w_self_hbm,
    w_neigh_hbm,
    bias_hbm,
    out_ref,
    targets_ref,
    near_ref,
    hot_ref,
    hot_req_ref,
    live_ref,
    table_ref,
    owner_ref,
    wanted_ref,
    w_self_ref,
    w_neigh_ref,
    bias_ref,
    ask,
    hot_ask,
    ids_a,
    ids_b,
    ids_c,
    hot_ids,
    square,
    hits,
    hits_x,
    z_out,
    z_in,
    y_out,
    y_in,
    x_out,
    x_in,
    row_out,
    row_in,
    extra,
    h_out,
    h_in,
    tally,
    summed,
    total,
    load_sem,
    send_ids,
    recv_ids,
    send_z,
    recv_z,
    send_y,
    recv_y,
    send_x,
    recv_x,
    send_h,
    recv_h,
):
    group, member = lax.axis_index("group"), lax.axis_index("member")
    z, yc = group // nyc, group % nyc
    ngroup = nz * nyc
    owned, features = table_ref.shape
    width = features // CHUNKS
    slots = h_out.shape[0] // nm
    hot_slots = nm * slots
    rows = targets_ref.shape[0]
    bf16, f32, i32 = jnp.bfloat16, jnp.float32, jnp.int32

    def iota(shape, dim):
        return lax.broadcasted_iota(i32, shape, dim)

    def z_peer(step):
        far = nz // 2 - (step + 1) // 2
        return (z + nz + (1 - 2 * (step % 2)) * far) % nz

    def yc_peer(step):
        return (yc + 1 + step) % nyc

    def m_peer(step):
        return (member + 1 + step) % nm

    def to_z(peer):
        return (peer * nyc + yc, member)

    def to_yc(peer):
        return (z * nyc + peer, member)

    def to_m(peer):
        return (group, peer)

    def each(count, body):
        lax.fori_loop(0, count, lambda i, c: (body(i), c)[1], 0)

    def send(source, target, send_sem, recv_sem, device):
        pltpu.make_async_remote_copy(
            src_ref=source, dst_ref=target, send_sem=send_sem, recv_sem=recv_sem, device_id=device, device_id_type=MESH
        ).start()

    def block(peer, count):
        return pl.ds(pl.multiple_of(peer * count, count), count)

    loads = [
        pltpu.make_async_copy(source, target, load_sem.at[number])
        for number, (source, target) in enumerate(
            [
                (owner_hbm, owner_ref),
                (wanted_hbm, wanted_ref),
                (hot_req_hbm, hot_req_ref),
                (live_hbm, live_ref),
                (bias_hbm, bias_ref),
                (hot_hbm, hot_ref),
                (table_hbm, table_ref),
                (near_hbm, near_ref),
                (targets_hbm, targets_ref),
                (w_self_hbm, w_self_ref),
                (w_neigh_hbm, w_neigh_ref),
            ]
        )
    ]
    for load in loads:
        load.start()

    barrier = pltpu.get_barrier_semaphore()

    def greet(device):
        pl.semaphore_signal(barrier, inc=1, device_id=device, device_id_type=MESH)

    each(nyc - 1, lambda i: greet(to_yc(yc_peer(i))))
    each(nz - 1, lambda i: greet(to_z(z_peer(i))))
    each(nm - 1, lambda i: greet(to_m(m_peer(i))))

    for load in loads[:3]:
        load.wait()
    requests = owner_ref.shape[-1]
    owners = owner_ref[0]
    coded = iota((1, requests), 1) * owned + wanted_ref[0]
    asked = jnp.broadcast_to(owners, (ngroup, requests)) == iota((ngroup, requests), 0)
    coded = jnp.broadcast_to(coded, (ngroup, requests))
    first = jnp.min(jnp.where(asked, coded, requests * owned), axis=1, keepdims=True)
    last = jnp.max(jnp.where(asked, coded, -1), axis=1, keepdims=True)
    twice = last > first
    first_row = jnp.where(first < requests * owned, lax.rem(first, owned), 0)
    last_row = jnp.where(twice, lax.rem(last, owned), -1)
    lane = iota((nyc, LANES), 1)
    packed = jnp.zeros((nyc, LANES), i32)
    for peer in range(nz):
        part = slice(peer * nyc, (peer + 1) * nyc)
        packed = jnp.where(lane == peer, first_row[part], packed)
        packed = jnp.where(lane == nz + peer, last_row[part], packed)
    for peer in range(nyc):
        ask[peer] = packed[peer : peer + 1]
    for peer in range(nm):
        hot_ask[peer] = jnp.zeros((1, LANES), i32)
        hot_ask[peer, :, 0:slots] = hot_req_ref[0, 0, peer : peer + 1, :]

    pl.semaphore_wait(barrier, nz + nyc + nm - 3)

    def send_ids_yc(i):
        peer = yc_peer(i)
        send(ask.at[peer], ids_a.at[yc], send_ids.at[0], recv_ids.at[0], to_yc(peer))

    each(nyc - 1, send_ids_yc)

    def send_ids_m(i):
        peer = m_peer(i)
        send(hot_ask.at[peer], hot_ids.at[member], send_ids.at[2], recv_ids.at[2], to_m(peer))

    each(nm - 1, send_ids_m)
    ids_a[yc] = ask[yc]
    hot_ids[member] = hot_ask[member]
    square[...] = jnp.zeros_like(square)

    wait_bytes(ids_a.at[pl.ds(0, nyc - 1)], recv_ids.at[0])
    for peer in range(nyc):
        square[peer : peer + 1, :] = ids_a[peer]
    square[...] = square[...].T
    for peer in range(nz):
        ids_b[peer, :, 0:nyc] = square[peer : peer + 1, 0:nyc]
        ids_b[peer, :, nyc : 2 * nyc] = square[nz + peer : nz + peer + 1, 0:nyc]

    def send_ids_z(i):
        peer = z_peer(i)
        send(ids_b.at[peer], ids_c.at[z], send_ids.at[1], recv_ids.at[1], to_z(peer))

    each(nz - 1, send_ids_z)
    ids_c[z] = ids_b[z]

    wait_bytes(hot_ids.at[pl.ds(0, nm - 1)], recv_ids.at[2])
    loads[5].wait()
    for peer in range(nm):
        wanted_rows = one_hot(lane_to_rows(hot_ids[peer], slots, 0), hot_ref.shape[0])
        h_out[peer * slots : (peer + 1) * slots, :] = exact_dot(wanted_rows, hot_ref[...]).astype(bf16)

    def send_hot(i):
        peer = m_peer(i)
        send(h_out.at[block(peer, slots)], h_in.at[block(member, slots)], send_h, recv_h, to_m(peer))

    each(nm - 1, send_hot)
    h_in[block(member, slots), :] = h_out[block(member, slots), :]

    rows_to = iota((ngroup, ngroup), 0)
    rows_from = iota((ngroup, ngroup), 1)
    turn = (rows_from == lax.rem(rows_to, nz) * nyc + lax.div(rows_to, nz)).astype(f32).astype(bf16)

    loads[6].wait()
    wait_bytes(ids_c.at[pl.ds(0, nz - 1)], recv_ids.at[1])
    for peer in range(nz):
        hits[peer * nyc : (peer + 1) * nyc, :] = one_hot(lane_to_rows(ids_c[peer], nyc, 0), owned)

    def gather_and_send(chunk):
        z_out[chunk] = exact_dot(hits[...], table_ref[:, chunk * width : (chunk + 1) * width]).astype(bf16)

        def send_rows(i):
            peer = z_peer(i)
            send(
                z_out.at[chunk, block(peer, nyc)],
                z_in.at[chunk, block(z, nyc)],
                send_z.at[chunk],
                recv_z.at[chunk],
                to_z(peer),
            )

        each(nz - 1, send_rows)
        z_in[chunk, block(z, nyc), :] = z_out[chunk, block(z, nyc), :]

    gather_and_send(0)

    for peer in range(nz):
        hits_x[peer * nyc : (peer + 1) * nyc, :] = one_hot(lane_to_rows(ids_c[peer], nyc, nyc), owned)
    ordered = exact_dot(turn, hits_x[...]).astype(bf16)
    x_out[...] = exact_dot(ordered, table_ref[...]).astype(bf16)

    def send_extra(i):
        peer = yc_peer(i)
        send(x_out.at[block(peer, nz)], x_in.at[block(yc, nz)], send_x.at[0], recv_x.at[0], to_yc(peer))

    each(nyc - 1, send_extra)
    x_in[block(yc, nz), :] = x_out[block(yc, nz), :]

    for chunk in range(1, CHUNKS):
        gather_and_send(chunk)

    def turn_and_send(chunk):
        wait_bytes(z_in.at[chunk, pl.ds(0, (nz - 1) * nyc)], recv_z.at[chunk])
        y_out[chunk] = exact_dot(turn, z_in[chunk]).astype(bf16)

        def send_rows(i):
            peer = yc_peer(i)
            send(
                y_out.at[chunk, block(peer, nz)],
                y_in.at[chunk, block(yc, nz)],
                send_y.at[chunk],
                recv_y.at[chunk],
                to_yc(peer),
            )

        each(nyc - 1, send_rows)
        y_in[chunk, block(yc, nz), :] = y_out[chunk, block(yc, nz), :]

    loads[7].wait()
    loads[3].wait()
    for first_slot in range(0, tally.shape[0], LANES):
        span = min(LANES, tally.shape[0] - first_slot)
        numbers = iota((span, rows), 0) + first_slot
        counted = jnp.zeros((span, rows), f32)
        for j in range(near_ref.shape[0]):
            counted = counted + jnp.where(near_ref[j : j + 1, :] == numbers, 1.0, 0.0)
        tally[first_slot : first_slot + span, :] = counted
    slot = iota((hot_slots, 1), 0)
    limit = jnp.zeros((hot_slots, 1), i32)
    for peer in range(nm):
        limit = jnp.where(lax.div(slot, slots) == peer, live_ref[0, :, peer : peer + 1], limit)
    hot_tally = jnp.where(lax.rem(slot, slots) < limit, tally[0:hot_slots, :], 0.0).astype(bf16)
    cold_tally = tally[hot_slots:, :]
    position = iota((ngroup, requests), 1)
    place = (position == lax.div(first, owned)).astype(f32).astype(bf16)
    place = exact_dot(turn, place).astype(bf16)
    placed = exact_dot(place, cold_tally.astype(bf16)).astype(bf16)
    last_at = jnp.max(jnp.where(twice, lax.div(last, owned), -1), axis=0, keepdims=True)
    second = jnp.sum(jnp.where(iota((requests, 1), 0) == last_at, cold_tally, 0.0), axis=0, keepdims=True)
    second = jnp.broadcast_to(second, (nz, rows)).astype(bf16)

    for load in loads[8:10]:
        load.wait()
    loads[4].wait()
    total[...] = exact_dot(targets_ref[...], w_self_ref[...]) + bias_ref[...].reshape(1, -1)

    turn_and_send(0)

    wait_bytes(x_in.at[pl.ds(0, (nyc - 1) * nz)], recv_x.at[0])
    target = iota((nz, ngroup), 0)
    source = iota((nz, ngroup), 1)
    pick = (lax.rem(source, nz) == target).astype(f32).astype(bf16)
    picked = exact_dot(pick, x_in[...])
    for peer in range(nz):
        row_out[peer] = picked[peer : peer + 1, :]

    def send_extra_row(i):
        peer = z_peer(i)
        send(row_out.at[peer], row_in.at[z], send_x.at[1], recv_x.at[1], to_z(peer))

    each(nz - 1, send_extra_row)
    row_in[z] = row_out[z]

    wait_bytes(h_in.at[pl.ds(0, (nm - 1) * slots)], recv_h)
    summed[...] = count_dot(hot_tally, h_in[...])

    for chunk in range(1, CHUNKS):
        turn_and_send(chunk)

    wait_bytes(row_in.at[pl.ds(0, nz - 1)], recv_x.at[1])
    for peer in range(nz):
        extra[peer : peer + 1, :] = row_in[peer]
    summed[...] = summed[...] + count_dot(second, extra[...].astype(bf16))
    loads[10].wait()
    for chunk in range(CHUNKS):
        part = slice(chunk * width, (chunk + 1) * width)
        wait_bytes(y_in.at[chunk, pl.ds(0, (nyc - 1) * nz)], recv_y.at[chunk])
        aggregate = summed[:, part] + count_dot(placed, y_in[chunk])
        aggregate = (aggregate * (1.0 / FANOUT)).astype(bf16)
        total[...] = total[...] + exact_dot(aggregate, w_neigh_ref[part, :])
    active = jnp.maximum(total[...], 0.0)
    scale = lax.rsqrt(jnp.mean(active * active, axis=-1, keepdims=True) + 1e-06)
    out_ref[...] = (active * scale).astype(bf16)

    wait_bytes(ids_a.at[pl.ds(0, nyc - 1)], send_ids.at[0])
    wait_bytes(ids_c.at[pl.ds(0, nz - 1)], send_ids.at[1])
    wait_bytes(hot_ids.at[pl.ds(0, nm - 1)], send_ids.at[2])
    wait_bytes(h_in.at[pl.ds(0, (nm - 1) * slots)], send_h)
    wait_bytes(x_in.at[pl.ds(0, (nyc - 1) * nz)], send_x.at[0])
    wait_bytes(row_in.at[pl.ds(0, nz - 1)], send_x.at[1])
    for chunk in range(CHUNKS):
        wait_bytes(z_in.at[chunk, pl.ds(0, (nz - 1) * nyc)], send_z.at[chunk])
        wait_bytes(y_in.at[chunk, pl.ds(0, (nyc - 1) * nz)], send_y.at[chunk])


def per_device(nz, nyc, *args):
    targets, near, hot_table, hot_req, live, cold_table, owner, wanted, w_self, w_neigh, bias = args
    args = (targets, near.T) + args[2:]
    nm, slots = hot_req.shape[2:]
    ngroup = nz * nyc
    owned, features = cold_table.shape
    rows, hidden = targets.shape[0], w_self.shape[1]
    bf16, f32, i32 = jnp.bfloat16, jnp.float32, jnp.int32
    chunked = pltpu.VMEM((CHUNKS, ngroup, features // CHUNKS), bf16)
    dma = pltpu.SemaphoreType.DMA
    return pl.pallas_call(
        functools.partial(layer_kernel, nz, nyc, nm),
        out_shape=jax.ShapeDtypeStruct((rows, hidden), bf16),
        in_specs=[pl.BlockSpec(memory_space=pltpu.HBM)] * len(args),
        out_specs=pl.BlockSpec(memory_space=pltpu.VMEM),
        scratch_shapes=[pltpu.VMEM(a.shape, a.dtype) for a in args]
        + [
            pltpu.VMEM((nyc, 1, LANES), i32),
            pltpu.VMEM((nm, 1, LANES), i32),
            pltpu.VMEM((nyc, 1, LANES), i32),
            pltpu.VMEM((nz, 1, LANES), i32),
            pltpu.VMEM((nz, 1, LANES), i32),
            pltpu.VMEM((nm, 1, LANES), i32),
            pltpu.VMEM((LANES, LANES), i32),
            pltpu.VMEM((ngroup, owned), bf16),
            pltpu.VMEM((ngroup, owned), bf16),
            chunked,
            chunked,
            chunked,
            chunked,
            pltpu.VMEM((ngroup, features), bf16),
            pltpu.VMEM((ngroup, features), bf16),
            pltpu.VMEM((nz, 1, features), f32),
            pltpu.VMEM((nz, 1, features), f32),
            pltpu.VMEM((nz, features), f32),
            pltpu.VMEM((nm * slots, features), bf16),
            pltpu.VMEM((nm * slots, features), bf16),
            pltpu.VMEM((nm * slots + owner.shape[-1], rows), f32),
            pltpu.VMEM((rows, features), f32),
            pltpu.VMEM((rows, hidden), f32),
            dma((len(args),)),
            dma((3,)),
            dma((3,)),
            dma((CHUNKS,)),
            dma((CHUNKS,)),
            dma((CHUNKS,)),
            dma((CHUNKS,)),
            dma((2,)),
            dma((2,)),
            dma,
            dma,
        ],
        compiler_params=pltpu.CompilerParams(
            collective_id=0, has_side_effects=True, vmem_limit_bytes=60 * 1024 * 1024
        ),
        cost_estimate=pl.CostEstimate(
            flops=4 * rows * features * hidden, bytes_accessed=8 * 1024 * 1024, transcendentals=rows
        ),
    )(*args)


def solution(mesh, nyc=16):
    nz = mesh.shape["group"] // nyc
    return jax.shard_map(
        functools.partial(per_device, nz, nyc),
        mesh=mesh,
        in_specs=(
            P(("group", "member"), None),
            P(("group", "member"), None),
            P("member", None),
            P("group", "member", None, None),
            P("group", "member", None),
            P("group", None),
            P("group", "member", None),
            P("group", "member", None),
            P(),
            P(),
            P(),
        ),
        out_specs=P(("group", "member"), None),
        check_vma=False,
    )
```

```python
import functools

import jax
import jax.numpy as jnp
from jax import lax
from jax.experimental import pallas as pl
from jax.experimental.pallas import tpu as pltpu
from jax.sharding import PartitionSpec as P

FANOUT = 25
LANES = 128
CHUNKS = 3
MESH = pl.DeviceIdType.MESH


def wait_bytes(ref, sem):
    pltpu.make_async_copy(ref, ref, sem).wait()


def one_hot(index, width):
    columns = lax.broadcasted_iota(jnp.int32, (index.shape[0], width), 1)
    return (columns == index).astype(jnp.float32).astype(jnp.bfloat16)


def lane_to_rows(row, rows, first):
    wide = jnp.broadcast_to(row, (rows, LANES))
    lane = lax.broadcasted_iota(jnp.int32, (rows, LANES), 1)
    slot = lax.broadcasted_iota(jnp.int32, (rows, LANES), 0)
    return jnp.sum(jnp.where(lane == slot + first, wide, 0), axis=1, keepdims=True)


def exact_dot(a, b):
    return jnp.dot(a, b, preferred_element_type=jnp.float32)


def count_dot(counts, values):
    return lax.dot_general(counts, values, (((0,), (0,)), ((), ())), preferred_element_type=jnp.float32)


def layer_kernel(
    nz,
    nyc,
    nm,
    targets_hbm,
    near_hbm,
    hot_hbm,
    hot_req_hbm,
    live_hbm,
    table_hbm,
    owner_hbm,
    wanted_hbm,
    w_self_hbm,
    w_neigh_hbm,
    bias_hbm,
    out_ref,
    targets_ref,
    near_ref,
    hot_ref,
    hot_req_ref,
    live_ref,
    table_ref,
    owner_ref,
    wanted_ref,
    w_self_ref,
    w_neigh_ref,
    bias_ref,
    ask,
    hot_ask,
    ids_a,
    ids_b,
    ids_c,
    hot_ids,
    square,
    near_ids,
    hits,
    z_out,
    z_in,
    y_out,
    y_in,
    x_out,
    x_in,
    row_out,
    row_in,
    extra,
    h_out,
    h_in,
    tally,
    summed,
    total,
    load_sem,
    send_ids,
    recv_ids,
    send_z,
    recv_z,
    send_y,
    recv_y,
    send_x,
    recv_x,
    send_h,
    recv_h,
):
    group, member = lax.axis_index("group"), lax.axis_index("member")
    z, yc = group // nyc, group % nyc
    ngroup = nz * nyc
    owned, features = table_ref.shape
    width = features // CHUNKS
    slots = h_out.shape[0] // nm
    hot_slots = nm * slots
    rows = targets_ref.shape[0]
    bf16, f32, i32 = jnp.bfloat16, jnp.float32, jnp.int32

    def iota(shape, dim):
        return lax.broadcasted_iota(i32, shape, dim)

    def z_peer(step):
        far = nz // 2 - (step + 1) // 2
        return (z + nz + (1 - 2 * (step % 2)) * far) % nz

    def yc_peer(step):
        return (yc + 1 + step) % nyc

    def m_peer(step):
        return (member + 1 + step) % nm

    def to_z(peer):
        return (peer * nyc + yc, member)

    def to_yc(peer):
        return (z * nyc + peer, member)

    def to_m(peer):
        return (group, peer)

    def each(count, body):
        lax.fori_loop(0, count, lambda i, c: (body(i), c)[1], 0)

    def send(source, target, send_sem, recv_sem, device):
        pltpu.make_async_remote_copy(
            src_ref=source, dst_ref=target, send_sem=send_sem, recv_sem=recv_sem, device_id=device, device_id_type=MESH
        ).start()

    def block(peer, count):
        return pl.ds(pl.multiple_of(peer * count, count), count)

    loads = [
        pltpu.make_async_copy(source, target, load_sem.at[number])
        for number, (source, target) in enumerate(
            [
                (owner_hbm, owner_ref),
                (wanted_hbm, wanted_ref),
                (hot_req_hbm, hot_req_ref),
                (live_hbm, live_ref),
                (bias_hbm, bias_ref),
                (hot_hbm, hot_ref),
                (table_hbm, table_ref),
                (near_hbm, near_ref),
                (targets_hbm, targets_ref),
                (w_self_hbm, w_self_ref),
                (w_neigh_hbm, w_neigh_ref),
            ]
        )
    ]
    for load in loads:
        load.start()

    barrier = pltpu.get_barrier_semaphore()

    def greet(device):
        pl.semaphore_signal(barrier, inc=1, device_id=device, device_id_type=MESH)

    each(nz - 1, lambda i: greet(to_z(z_peer(i))))
    each(nyc - 1, lambda i: greet(to_yc(yc_peer(i))))
    each(nm - 1, lambda i: greet(to_m(m_peer(i))))

    for load in loads[:3]:
        load.wait()
    requests = owner_ref.shape[-1]
    owners = owner_ref[0]
    coded = iota((1, requests), 1) * owned + wanted_ref[0]
    asked = jnp.broadcast_to(owners, (ngroup, requests)) == iota((ngroup, requests), 0)
    coded = jnp.broadcast_to(coded, (ngroup, requests))
    first = jnp.min(jnp.where(asked, coded, requests * owned), axis=1, keepdims=True)
    last = jnp.max(jnp.where(asked, coded, -1), axis=1, keepdims=True)
    twice = last > first
    first_row = jnp.where(first < requests * owned, lax.rem(first, owned), 0)
    last_row = jnp.where(twice, lax.rem(last, owned), -1)
    lane = iota((nyc, LANES), 1)
    slot = iota((nyc, LANES), 0)
    for peer in range(nz):
        part = slice(peer * nyc, (peer + 1) * nyc)
        packed = jnp.where(lane == slot, first_row[part], 0) + jnp.where(lane == slot + nyc, last_row[part], 0)
        ask[peer] = jnp.sum(packed, axis=0, keepdims=True)
    for peer in range(nm):
        hot_ask[peer] = jnp.zeros((1, LANES), i32)
        hot_ask[peer, :, 0:slots] = hot_req_ref[0, 0, peer : peer + 1, :]

    pl.semaphore_wait(barrier, nz + nyc + nm - 3)

    def send_ids_z(i):
        peer = z_peer(i)
        send(ask.at[peer], ids_a.at[z], send_ids.at[0], recv_ids.at[0], to_z(peer))

    each(nz - 1, send_ids_z)

    def send_ids_m(i):
        peer = m_peer(i)
        send(hot_ask.at[peer], hot_ids.at[member], send_ids.at[2], recv_ids.at[2], to_m(peer))

    each(nm - 1, send_ids_m)
    ids_a[z] = ask[z]
    hot_ids[member] = hot_ask[member]
    square[...] = jnp.zeros_like(square)

    loads[7].wait()
    loads[3].wait()
    for first_slot in range(0, tally.shape[0], LANES):
        span = min(LANES, tally.shape[0] - first_slot)
        numbers = iota((span, rows), 0) + first_slot
        counted = jnp.zeros((span, rows), f32)
        for j in range(near_ref.shape[0]):
            counted = counted + jnp.where(near_ref[j : j + 1, :] == numbers, 1.0, 0.0)
        tally[first_slot : first_slot + span, :] = counted
    slot = iota((hot_slots, 1), 0)
    limit = jnp.zeros((hot_slots, 1), i32)
    for peer in range(nm):
        limit = jnp.where(lax.div(slot, slots) == peer, live_ref[0, :, peer : peer + 1], limit)
    hot_tally = jnp.where(lax.rem(slot, slots) < limit, tally[0:hot_slots, :], 0.0).astype(bf16)
    cold_tally = tally[hot_slots:, :]

    wait_bytes(hot_ids.at[pl.ds(0, nm - 1)], recv_ids.at[2])
    loads[5].wait()
    for peer in range(nm):
        wanted_rows = one_hot(lane_to_rows(hot_ids[peer], slots, 0), hot_ref.shape[0])
        h_out[peer * slots : (peer + 1) * slots, :] = exact_dot(wanted_rows, hot_ref[...]).astype(bf16)

    def send_hot(i):
        peer = m_peer(i)
        send(h_out.at[block(peer, slots)], h_in.at[block(member, slots)], send_h, recv_h, to_m(peer))

    each(nm - 1, send_hot)
    h_in[block(member, slots), :] = h_out[block(member, slots), :]

    wait_bytes(ids_a.at[pl.ds(0, nz - 1)], recv_ids.at[0])
    for peer in range(nz):
        square[peer : peer + 1, :] = ids_a[peer]
    square[...] = square[...].T
    for peer in range(nyc):
        ids_b[peer, :, 0:nz] = square[peer : peer + 1, 0:nz]
        ids_b[peer, :, nz : 2 * nz] = square[nyc + peer : nyc + peer + 1, 0:nz]

    def send_ids_yc(i):
        peer = yc_peer(i)
        send(ids_b.at[peer], ids_c.at[yc], send_ids.at[1], recv_ids.at[1], to_yc(peer))

    each(nyc - 1, send_ids_yc)
    ids_c[yc] = ids_b[yc]

    rows_to = iota((ngroup, ngroup), 0)
    rows_from = iota((ngroup, ngroup), 1)
    turn = (rows_from == lax.rem(rows_to, nz) * nyc + lax.div(rows_to, nz)).astype(f32).astype(bf16)
    turn_back = (rows_from == lax.rem(rows_to, nyc) * nz + lax.div(rows_to, nyc)).astype(f32).astype(bf16)

    loads[6].wait()
    wait_bytes(ids_c.at[pl.ds(0, nyc - 1)], recv_ids.at[1])
    for peer in range(nyc):
        near_ids[peer : peer + 1, :] = ids_c[peer]
    for peer in range(nz):
        hits[peer * nyc : (peer + 1) * nyc, :] = one_hot(near_ids[:, peer : peer + 1], owned)

    def rows_along_z(chunk, rows_out):
        z_out[chunk] = rows_out.astype(bf16)

        def send_rows(i):
            peer = z_peer(i)
            send(
                z_out.at[chunk, block(peer, nyc)],
                z_in.at[chunk, block(z, nyc)],
                send_z.at[chunk],
                recv_z.at[chunk],
                to_z(peer),
            )

        each(nz - 1, send_rows)
        z_in[chunk, block(z, nyc), :] = z_out[chunk, block(z, nyc), :]

    def rows_along_y(chunk, rows_out):
        y_out[chunk] = rows_out.astype(bf16)

        def send_rows(i):
            peer = yc_peer(i)
            send(
                y_out.at[chunk, block(peer, nz)],
                y_in.at[chunk, block(yc, nz)],
                send_y.at[chunk],
                recv_y.at[chunk],
                to_yc(peer),
            )

        each(nyc - 1, send_rows)
        y_in[chunk, block(yc, nz), :] = y_out[chunk, block(yc, nz), :]

    def wait_z(chunk):
        wait_bytes(z_in.at[chunk, pl.ds(0, (nz - 1) * nyc)], recv_z.at[chunk])

    def wait_y(chunk):
        wait_bytes(y_in.at[chunk, pl.ds(0, (nyc - 1) * nz)], recv_y.at[chunk])

    def features_of(chunk):
        return slice(chunk * width, (chunk + 1) * width)

    final = CHUNKS - 1
    rows_along_z(0, exact_dot(hits[...], table_ref[:, features_of(0)]))
    turned = exact_dot(turn, hits[...]).astype(bf16)
    rows_along_y(final, exact_dot(turned, table_ref[:, features_of(final)]))

    for peer in range(nyc):
        hits[peer * nz : (peer + 1) * nz, :] = one_hot(lane_to_rows(ids_c[peer], nz, nz), owned)
    x_out[...] = exact_dot(hits[...], table_ref[...]).astype(bf16)

    def send_extra(i):
        peer = yc_peer(i)
        send(x_out.at[block(peer, nz)], x_in.at[block(yc, nz)], send_x.at[0], recv_x.at[0], to_yc(peer))

    each(nyc - 1, send_extra)
    x_in[block(yc, nz), :] = x_out[block(yc, nz), :]

    for peer in range(nz):
        hits[peer * nyc : (peer + 1) * nyc, :] = one_hot(near_ids[:, peer : peer + 1], owned)
    for chunk in range(1, final):
        rows_along_z(chunk, exact_dot(hits[...], table_ref[:, features_of(chunk)]))

    position = iota((ngroup, requests), 1)
    place = (position == lax.div(first, owned)).astype(f32).astype(bf16)
    placed = exact_dot(place, cold_tally.astype(bf16)).astype(bf16)
    placed_turned = exact_dot(turn, placed).astype(bf16)
    last_at = jnp.max(jnp.where(twice, lax.div(last, owned), -1), axis=0, keepdims=True)
    second = jnp.sum(jnp.where(iota((requests, 1), 0) == last_at, cold_tally, 0.0), axis=0, keepdims=True)
    second = jnp.broadcast_to(second, (nz, rows)).astype(bf16)

    for load in loads[8:10]:
        load.wait()
    loads[4].wait()
    total[...] = exact_dot(targets_ref[...], w_self_ref[...]) + bias_ref[...].reshape(1, -1)

    wait_z(0)
    rows_along_y(0, exact_dot(turn, z_in[0]))
    wait_y(final)
    rows_along_z(final, exact_dot(turn_back, y_in[final]))

    wait_bytes(x_in.at[pl.ds(0, (nyc - 1) * nz)], recv_x.at[0])
    target = iota((nz, ngroup), 0)
    source = iota((nz, ngroup), 1)
    pick = (lax.rem(source, nz) == target).astype(f32).astype(bf16)
    picked = exact_dot(pick, x_in[...])
    for peer in range(nz):
        row_out[peer] = picked[peer : peer + 1, :]

    def send_extra_row(i):
        peer = z_peer(i)
        send(row_out.at[peer], row_in.at[z], send_x.at[1], recv_x.at[1], to_z(peer))

    each(nz - 1, send_extra_row)
    row_in[z] = row_out[z]

    wait_bytes(h_in.at[pl.ds(0, (nm - 1) * slots)], recv_h)
    summed[...] = count_dot(hot_tally, h_in[...])

    for chunk in range(1, final):
        wait_z(chunk)
        rows_along_y(chunk, exact_dot(turn, z_in[chunk]))

    loads[10].wait()

    def add_chunk(chunk, counts, rows_in):
        part = features_of(chunk)
        aggregate = summed[:, part] + count_dot(counts, rows_in)
        aggregate = (aggregate * (1.0 / FANOUT)).astype(bf16)
        total[...] = total[...] + exact_dot(aggregate, w_neigh_ref[part, :])

    wait_bytes(row_in.at[pl.ds(0, nz - 1)], recv_x.at[1])
    for peer in range(nz):
        extra[peer : peer + 1, :] = row_in[peer]
    summed[...] = summed[...] + count_dot(second, extra[...].astype(bf16))
    for chunk in range(final):
        wait_y(chunk)
        add_chunk(chunk, placed_turned, y_in[chunk])
    wait_z(final)
    add_chunk(final, placed, z_in[final])
    active = jnp.maximum(total[...], 0.0)
    scale = lax.rsqrt(jnp.mean(active * active, axis=-1, keepdims=True) + 1e-06)
    out_ref[...] = (active * scale).astype(bf16)

    wait_bytes(ids_a.at[pl.ds(0, nz - 1)], send_ids.at[0])
    wait_bytes(ids_c.at[pl.ds(0, nyc - 1)], send_ids.at[1])
    wait_bytes(hot_ids.at[pl.ds(0, nm - 1)], send_ids.at[2])
    wait_bytes(h_in.at[pl.ds(0, (nm - 1) * slots)], send_h)
    wait_bytes(x_in.at[pl.ds(0, (nyc - 1) * nz)], send_x.at[0])
    wait_bytes(row_in.at[pl.ds(0, nz - 1)], send_x.at[1])
    for chunk in range(CHUNKS):
        wait_bytes(z_in.at[chunk, pl.ds(0, (nz - 1) * nyc)], send_z.at[chunk])
        wait_bytes(y_in.at[chunk, pl.ds(0, (nyc - 1) * nz)], send_y.at[chunk])


def per_device(nz, nyc, *args):
    targets, near, hot_table, hot_req, live, cold_table, owner, wanted, w_self, w_neigh, bias = args
    args = (targets, near.T) + args[2:]
    nm, slots = hot_req.shape[2:]
    ngroup = nz * nyc
    owned, features = cold_table.shape
    rows, hidden = targets.shape[0], w_self.shape[1]
    bf16, f32, i32 = jnp.bfloat16, jnp.float32, jnp.int32
    chunked = pltpu.VMEM((CHUNKS, ngroup, features // CHUNKS), bf16)
    dma = pltpu.SemaphoreType.DMA
    return pl.pallas_call(
        functools.partial(layer_kernel, nz, nyc, nm),
        out_shape=pltpu.VMEM((rows, hidden), bf16),
        in_specs=[pl.BlockSpec(memory_space=pltpu.HBM)] * len(args),
        out_specs=pl.BlockSpec(memory_space=pltpu.VMEM),
        scratch_shapes=[pltpu.VMEM(a.shape, a.dtype) for a in args]
        + [
            pltpu.VMEM((nz, 1, LANES), i32),
            pltpu.VMEM((nm, 1, LANES), i32),
            pltpu.VMEM((nz, 1, LANES), i32),
            pltpu.VMEM((nyc, 1, LANES), i32),
            pltpu.VMEM((nyc, 1, LANES), i32),
            pltpu.VMEM((nm, 1, LANES), i32),
            pltpu.VMEM((LANES, LANES), i32),
            pltpu.VMEM((nyc, LANES), i32),
            pltpu.VMEM((ngroup, owned), bf16),
            chunked,
            chunked,
            chunked,
            chunked,
            pltpu.VMEM((ngroup, features), bf16),
            pltpu.VMEM((ngroup, features), bf16),
            pltpu.VMEM((nz, 1, features), f32),
            pltpu.VMEM((nz, 1, features), f32),
            pltpu.VMEM((nz, features), f32),
            pltpu.VMEM((nm * slots, features), bf16),
            pltpu.VMEM((nm * slots, features), bf16),
            pltpu.VMEM((nm * slots + owner.shape[-1], rows), f32),
            pltpu.VMEM((rows, features), f32),
            pltpu.VMEM((rows, hidden), f32),
            dma((len(args),)),
            dma((3,)),
            dma((3,)),
            dma((CHUNKS,)),
            dma((CHUNKS,)),
            dma((CHUNKS,)),
            dma((CHUNKS,)),
            dma((2,)),
            dma((2,)),
            dma,
            dma,
        ],
        compiler_params=pltpu.CompilerParams(
            collective_id=0, has_side_effects=True, vmem_limit_bytes=60 * 1024 * 1024
        ),
        cost_estimate=pl.CostEstimate(
            flops=4 * rows * features * hidden, bytes_accessed=8 * 1024 * 1024, transcendentals=rows
        ),
    )(*args)


def solution(mesh, nyc=16):
    nz = mesh.shape["group"] // nyc
    return jax.shard_map(
        functools.partial(per_device, nz, nyc),
        mesh=mesh,
        in_specs=(
            P(("group", "member"), None),
            P(("group", "member"), None),
            P("member", None),
            P("group", "member", None, None),
            P("group", "member", None),
            P("group", None),
            P("group", "member", None),
            P("group", "member", None),
            P(),
            P(),
            P(),
        ),
        out_specs=P(("group", "member"), None),
        check_vma=False,
    )
```

```python
import functools

import jax
import jax.numpy as jnp
from jax import lax
from jax.experimental import pallas as pl
from jax.experimental.pallas import tpu as pltpu
from jax.sharding import PartitionSpec as P

FANOUT = 25
LANES = 128
PIECES = 6
Z_FIRST = ((0, 2), (2, 1))
Y_FIRST = ((3, 1), (4, 2))
MESH = pl.DeviceIdType.MESH


def wait_bytes(ref, sem):
    pltpu.make_async_copy(ref, ref, sem).wait()


def one_hot(index, width):
    columns = lax.broadcasted_iota(jnp.int32, (index.shape[0], width), 1)
    return (columns == index).astype(jnp.float32).astype(jnp.bfloat16)


def lane_to_rows(row, rows, first):
    wide = jnp.broadcast_to(row, (rows, LANES))
    lane = lax.broadcasted_iota(jnp.int32, (rows, LANES), 1)
    slot = lax.broadcasted_iota(jnp.int32, (rows, LANES), 0)
    return jnp.sum(jnp.where(lane == slot + first, wide, 0), axis=1, keepdims=True)


def exact_dot(a, b):
    return jnp.dot(a, b, preferred_element_type=jnp.float32)


def count_dot(counts, values):
    return lax.dot_general(counts, values, (((0,), (0,)), ((), ())), preferred_element_type=jnp.float32)


def layer_kernel(
    nz,
    nyc,
    nm,
    targets_hbm,
    near_hbm,
    hot_hbm,
    hot_req_hbm,
    live_hbm,
    table_hbm,
    owner_hbm,
    wanted_hbm,
    w_self_hbm,
    w_neigh_hbm,
    bias_hbm,
    out_ref,
    targets_ref,
    near_ref,
    hot_ref,
    hot_req_ref,
    live_ref,
    table_ref,
    owner_ref,
    wanted_ref,
    w_self_ref,
    w_neigh_ref,
    bias_ref,
    ask,
    hot_ask,
    ids_a,
    ids_b,
    ids_c,
    hot_ids,
    square,
    hits,
    hits_x,
    z_out,
    z_in,
    y_out,
    y_in,
    x_out,
    x_core,
    x_send,
    x_in,
    row_out,
    row_in,
    extra,
    h_out,
    h_in,
    tally,
    summed,
    total,
    load_sem,
    send_ids,
    recv_ids,
    recv_ids_z,
    send_z,
    recv_z,
    send_y,
    recv_y,
    send_x,
    recv_x,
    send_h,
    recv_h,
):
    group, member = lax.axis_index("group"), lax.axis_index("member")
    z, yc = group // nyc, group % nyc
    y, core, ny = yc // 2, yc % 2, nyc // 2
    ngroup = nz * nyc
    half = ny * nz
    owned, features = table_ref.shape
    width = features // PIECES
    slots = h_out.shape[0] // nm
    hot_slots = nm * slots
    rows = targets_ref.shape[0]
    bf16, f32, i32 = jnp.bfloat16, jnp.float32, jnp.int32

    def iota(shape, dim):
        return lax.broadcasted_iota(i32, shape, dim)

    def z_peer(step):
        far = nz // 2 - (step + 1) // 2
        return (z + nz + (1 - 2 * (step % 2)) * far) % nz

    def yc_peer(step):
        return (yc + 1 + step) % nyc

    def m_peer(step):
        return (member + 1 + step) % nm

    def to_z(peer):
        return (peer * nyc + yc, member)

    def to_yc(peer):
        return (z * nyc + peer, member)

    def to_m(peer):
        return (group, peer)

    def each(count, body):
        lax.fori_loop(0, count, lambda i, c: (body(i), c)[1], 0)

    def send(source, target, send_sem, recv_sem, device):
        pltpu.make_async_remote_copy(
            src_ref=source, dst_ref=target, send_sem=send_sem, recv_sem=recv_sem, device_id=device, device_id_type=MESH
        ).start()

    def block(peer, count):
        return pl.ds(pl.multiple_of(peer * count, count), count)

    loads = [
        pltpu.make_async_copy(source, target, load_sem.at[number])
        for number, (source, target) in enumerate(
            [
                (owner_hbm, owner_ref),
                (wanted_hbm, wanted_ref),
                (hot_req_hbm, hot_req_ref),
                (live_hbm, live_ref),
                (bias_hbm, bias_ref),
                (hot_hbm, hot_ref),
                (table_hbm, table_ref),
                (near_hbm, near_ref),
                (targets_hbm, targets_ref),
                (w_self_hbm, w_self_ref),
                (w_neigh_hbm, w_neigh_ref),
            ]
        )
    ]
    for load in loads:
        load.start()

    barrier = pltpu.get_barrier_semaphore()

    def greet(device):
        pl.semaphore_signal(barrier, inc=1, device_id=device, device_id_type=MESH)

    each(nz - 1, lambda i: greet(to_z(z_peer(i))))
    each(nyc - 1, lambda i: greet(to_yc(yc_peer(i))))
    each(nm - 1, lambda i: greet(to_m(m_peer(i))))

    for load in loads[:3]:
        load.wait()
    requests = owner_ref.shape[-1]
    owners = owner_ref[0]
    coded = iota((1, requests), 1) * owned + wanted_ref[0]
    asked = jnp.broadcast_to(owners, (ngroup, requests)) == iota((ngroup, requests), 0)
    coded = jnp.broadcast_to(coded, (ngroup, requests))
    first = jnp.min(jnp.where(asked, coded, requests * owned), axis=1, keepdims=True)
    last = jnp.max(jnp.where(asked, coded, -1), axis=1, keepdims=True)
    twice = last > first
    first_row = jnp.where(first < requests * owned, lax.rem(first, owned), 0)
    last_row = jnp.where(twice, lax.rem(last, owned), -1)
    lane = iota((nyc, LANES), 1)
    packed = jnp.zeros((nyc, LANES), i32)
    for peer in range(nz):
        part = slice(peer * nyc, (peer + 1) * nyc)
        packed = jnp.where(lane == peer, first_row[part], packed)
        packed = jnp.where(lane == nz + peer, last_row[part], packed)
    for peer in range(nyc):
        ask[peer] = packed[peer : peer + 1]
    for peer in range(nm):
        hot_ask[peer] = jnp.zeros((1, LANES), i32)
        hot_ask[peer, :, 0:slots] = hot_req_ref[0, 0, peer : peer + 1, :]

    pl.semaphore_wait(barrier, nz + nyc + nm - 3)

    def send_ids_yc(i):
        peer = yc_peer(i)
        send(ask.at[peer], ids_a.at[yc], send_ids.at[0], recv_ids.at[0], to_yc(peer))

    each(nyc - 1, send_ids_yc)

    def send_ids_m(i):
        peer = m_peer(i)
        send(hot_ask.at[peer], hot_ids.at[member], send_ids.at[2], recv_ids.at[2], to_m(peer))

    each(nm - 1, send_ids_m)
    ids_a[yc] = ask[yc]
    hot_ids[member] = hot_ask[member]
    square[...] = jnp.zeros_like(square)

    loads[7].wait()
    loads[3].wait()
    for first_slot in range(0, tally.shape[0], LANES):
        span = min(LANES, tally.shape[0] - first_slot)
        numbers = iota((span, rows), 0) + first_slot
        counted = jnp.zeros((span, rows), f32)
        for j in range(near_ref.shape[0]):
            counted = counted + jnp.where(near_ref[j : j + 1, :] == numbers, 1.0, 0.0)
        tally[first_slot : first_slot + span, :] = counted
    slot = iota((hot_slots, 1), 0)
    limit = jnp.zeros((hot_slots, 1), i32)
    for peer in range(nm):
        limit = jnp.where(lax.div(slot, slots) == peer, live_ref[0, :, peer : peer + 1], limit)
    hot_tally = jnp.where(lax.rem(slot, slots) < limit, tally[0:hot_slots, :], 0.0).astype(bf16)
    cold_tally = tally[hot_slots:, :]

    wait_bytes(hot_ids.at[pl.ds(0, nm - 1)], recv_ids.at[2])
    loads[5].wait()
    for peer in range(nm):
        wanted_rows = one_hot(lane_to_rows(hot_ids[peer], slots, 0), hot_ref.shape[0])
        h_out[peer * slots : (peer + 1) * slots, :] = exact_dot(wanted_rows, hot_ref[...]).astype(bf16)

    def send_hot(i):
        peer = m_peer(i)
        send(h_out.at[block(peer, slots)], h_in.at[block(member, slots)], send_h, recv_h, to_m(peer))

    each(nm - 1, send_hot)
    h_in[block(member, slots), :] = h_out[block(member, slots), :]

    wait_bytes(ids_a.at[pl.ds(0, nyc - 1)], recv_ids.at[0])
    for peer in range(nyc):
        square[peer : peer + 1, :] = ids_a[peer]
    square[...] = square[...].T
    for peer in range(nz):
        ids_b[peer, :, 0:nyc] = square[peer : peer + 1, 0:nyc]
        ids_b[peer, :, nyc : 2 * nyc] = square[nz + peer : nz + peer + 1, 0:nyc]

    def send_ids_z(i):
        peer = z_peer(i)
        send(ids_b.at[peer], ids_c.at[z], send_ids.at[1], recv_ids_z.at[z], to_z(peer))

    each(nz - 1, send_ids_z)
    ids_c[z] = ids_b[z]

    rows_to = iota((ngroup, ngroup), 0)
    rows_from = iota((ngroup, ngroup), 1)
    turn = (rows_from == lax.rem(rows_to, nz) * nyc + lax.div(rows_to, nz)).astype(f32).astype(bf16)
    turn_back = (rows_from == lax.rem(rows_to, nyc) * nz + lax.div(rows_to, nyc)).astype(f32).astype(bf16)

    loads[6].wait()
    def features_of(chunk):
        return slice(chunk[0] * width, (chunk[0] + chunk[1]) * width)

    def pieces_of(chunk):
        return pl.ds(chunk[0], chunk[1])

    def keep(ref, chunk, rows_of, values):
        for piece in range(chunk[1]):
            ref[chunk[0] + piece, rows_of, :] = values[:, piece * width : (piece + 1) * width].astype(bf16)

    def whole(ref, chunk):
        return jnp.concatenate([ref[chunk[0] + piece] for piece in range(chunk[1])], axis=1)

    offsets = [0]
    for far in range(1, nz // 2):
        offsets += [far, -far]
    offsets += [nz // 2]
    peers = [lax.rem(z + (nz + offset), nz) for offset in offsets]

    def send_batch(chunk, begin, end):
        for number in range(begin, end):
            held = pl.ds(number * nyc, nyc)
            if offsets[number]:
                send(
                    z_out.at[pieces_of(chunk), held],
                    z_in.at[pieces_of(chunk), block(z, nyc)],
                    send_z.at[chunk[0]],
                    recv_z.at[chunk[0]],
                    to_z(peers[number]),
                )
            else:
                z_in[pieces_of(chunk), block(z, nyc), :] = z_out[pieces_of(chunk), held, :]

    early = sum(count for _, count in Z_FIRST)
    cuts = [cut for cut in (0, 5, 9, 13) if cut < nz] + [nz]
    batches = list(zip(cuts[:-1], cuts[1:]))
    for begin, end in batches:
        wanted_rows = []
        for number in range(begin, end):
            peer = peers[number]
            if offsets[number]:
                wait_bytes(ids_c.at[peer], recv_ids_z.at[peer])
            row = ids_c[peer]
            wanted_rows.append(one_hot(lane_to_rows(row, nyc, 0), owned))
            hits[block(peer, nyc), :] = wanted_rows[-1]
            hits_x[block(peer, nyc), :] = one_hot(lane_to_rows(row, nyc, nyc), owned)
        found = exact_dot(jnp.concatenate(wanted_rows, axis=0), table_ref[:, 0 : early * width])
        keep(z_out, (0, early), slice(begin * nyc, end * nyc), found)
        send_batch(Z_FIRST[0], begin, end)
        if begin == 0:
            for chunk in Z_FIRST[1:]:
                send_batch(chunk, begin, end)

    def rows_along_z(chunk, rows_out):
        keep(z_out, chunk, slice(0, ngroup), rows_out)

        def send_rows(i):
            peer = z_peer(i)
            send(
                z_out.at[pieces_of(chunk), block(peer, nyc)],
                z_in.at[pieces_of(chunk), block(z, nyc)],
                send_z.at[chunk[0]],
                recv_z.at[chunk[0]],
                to_z(peer),
            )

        each(nz - 1, send_rows)
        z_in[pieces_of(chunk), block(z, nyc), :] = z_out[pieces_of(chunk), block(z, nyc), :]

    def rows_along_y(chunk, rows_out):
        keep(y_out, chunk, slice(0, ngroup), rows_out)

        def send_rows(i):
            peer = yc_peer(i)
            send(
                y_out.at[pieces_of(chunk), block(peer, nz)],
                y_in.at[pieces_of(chunk), block(yc, nz)],
                send_y.at[chunk[0]],
                recv_y.at[chunk[0]],
                to_yc(peer),
            )

        each(nyc - 1, send_rows)
        y_in[pieces_of(chunk), block(yc, nz), :] = y_out[pieces_of(chunk), block(yc, nz), :]

    def wait_z(chunk, sem=None):
        sem = recv_z if sem is None else sem
        wait_bytes(z_in.at[pieces_of(chunk), pl.ds(0, (nz - 1) * nyc)], sem.at[chunk[0]])

    def wait_y(chunk, sem=None):
        sem = recv_y if sem is None else sem
        wait_bytes(y_in.at[pieces_of(chunk), pl.ds(0, (nyc - 1) * nz)], sem.at[chunk[0]])

    turned = exact_dot(turn, hits[...]).astype(bf16)
    rows_along_y(Y_FIRST[0], exact_dot(turned, table_ref[:, features_of(Y_FIRST[0])]))
    for begin, end in batches[:0:-1]:
        for chunk in Z_FIRST[1:]:
            send_batch(chunk, begin, end)
    for chunk in Y_FIRST[1:]:
        rows_along_y(chunk, exact_dot(turned, table_ref[:, features_of(chunk)]))

    spread = (rows_from == lax.rem(rows_to, nz) * nyc + lax.rem(lax.div(rows_to, nz), ny) * 2 + lax.div(rows_to, half))
    spread = spread.astype(f32).astype(bf16)
    turned = exact_dot(spread, hits_x[...]).astype(bf16)
    x_out[...] = exact_dot(turned, table_ref[...]).astype(bf16)
    send(x_out.at[block(1 - core, half)], x_core, send_x.at[0], recv_x.at[0], to_yc(y * 2 + 1 - core))

    position = iota((ngroup, requests), 1)
    place = (position == lax.div(first, owned)).astype(f32).astype(bf16)
    placed = exact_dot(place, cold_tally.astype(bf16)).astype(bf16)
    placed_turned = exact_dot(turn, placed).astype(bf16)
    last_at = jnp.max(jnp.where(twice, lax.div(last, owned), -1), axis=0, keepdims=True)
    second = jnp.sum(jnp.where(iota((requests, 1), 0) == last_at, cold_tally, 0.0), axis=0, keepdims=True)
    second = jnp.broadcast_to(second, (nz, rows)).astype(bf16)

    wait_bytes(x_core, recv_x.at[0])
    x_send[...] = x_out[block(core, half), :] + x_core[...]

    def send_extra(i):
        peer = lax.rem(y + 1 + i, ny)
        send(x_send.at[block(peer, nz)], x_in.at[block(y, nz)], send_x.at[1], recv_x.at[1], to_yc(peer * 2 + core))

    each(ny - 1, send_extra)
    x_in[block(y, nz), :] = x_send[block(y, nz), :]

    for load in loads[8:10]:
        load.wait()
    loads[4].wait()
    total[...] = exact_dot(targets_ref[...], w_self_ref[...]) + bias_ref[...].reshape(1, -1)

    wait_y(Y_FIRST[0])
    rows_along_z(Y_FIRST[0], exact_dot(turn_back, whole(y_in, Y_FIRST[0])))
    wait_z(Z_FIRST[0])
    rows_along_y(Z_FIRST[0], exact_dot(turn, whole(z_in, Z_FIRST[0])))
    for chunk in Y_FIRST[1:]:
        wait_y(chunk)
        rows_along_z(chunk, exact_dot(turn_back, whole(y_in, chunk)))
    for chunk in Z_FIRST[1:]:
        wait_z(chunk)
        rows_along_y(chunk, exact_dot(turn, whole(z_in, chunk)))

    wait_bytes(x_in.at[pl.ds(0, (ny - 1) * nz)], recv_x.at[1])
    target = iota((nz, half), 0)
    source = iota((nz, half), 1)
    pick = (lax.rem(source, nz) == target).astype(f32).astype(bf16)
    picked = exact_dot(pick, x_in[...])
    for peer in range(nz):
        row_out[peer] = picked[peer : peer + 1, :]

    def send_extra_row(i):
        peer = z_peer(i)
        send(row_out.at[peer], row_in.at[z], send_x.at[2], recv_x.at[2], to_z(peer))

    each(nz - 1, send_extra_row)
    row_in[z] = row_out[z]

    wait_bytes(h_in.at[pl.ds(0, (nm - 1) * slots)], recv_h)
    summed[...] = count_dot(hot_tally, h_in[...])

    loads[10].wait()

    def add_chunk(chunk, counts, rows_in):
        part = features_of(chunk)
        aggregate = summed[:, part] + count_dot(counts, rows_in)
        aggregate = (aggregate * (1.0 / FANOUT)).astype(bf16)
        total[...] = total[...] + exact_dot(aggregate, w_neigh_ref[part, :])

    wait_bytes(row_in.at[pl.ds(0, nz - 1)], recv_x.at[2])
    for peer in range(nz):
        extra[peer : peer + 1, :] = row_in[peer]
    summed[...] = summed[...] + count_dot(second, extra[...].astype(bf16))
    wait_y(Z_FIRST[0])
    add_chunk(Z_FIRST[0], placed_turned, whole(y_in, Z_FIRST[0]))
    wait_z(Y_FIRST[0])
    add_chunk(Y_FIRST[0], placed, whole(z_in, Y_FIRST[0]))
    for chunk in Z_FIRST[1:]:
        wait_y(chunk)
        add_chunk(chunk, placed_turned, whole(y_in, chunk))
    for chunk in Y_FIRST[1:]:
        wait_z(chunk)
        add_chunk(chunk, placed, whole(z_in, chunk))
    active = jnp.maximum(total[...], 0.0)
    scale = lax.rsqrt(jnp.mean(active * active, axis=-1, keepdims=True) + 1e-06)
    out_ref[...] = (active * scale).astype(bf16)

    wait_bytes(ids_a.at[pl.ds(0, nyc - 1)], send_ids.at[0])
    wait_bytes(ids_c.at[pl.ds(0, nz - 1)], send_ids.at[1])
    wait_bytes(hot_ids.at[pl.ds(0, nm - 1)], send_ids.at[2])
    wait_bytes(h_in.at[pl.ds(0, (nm - 1) * slots)], send_h)
    wait_bytes(x_core, send_x.at[0])
    wait_bytes(x_in.at[pl.ds(0, (ny - 1) * nz)], send_x.at[1])
    wait_bytes(row_in.at[pl.ds(0, nz - 1)], send_x.at[2])
    for chunk in Z_FIRST + Y_FIRST:
        wait_z(chunk, send_z)
        wait_y(chunk, send_y)


def per_device(nz, nyc, *args):
    targets, near, hot_table, hot_req, live, cold_table, owner, wanted, w_self, w_neigh, bias = args
    args = (targets, near.T) + args[2:]
    nm, slots = hot_req.shape[2:]
    ngroup = nz * nyc
    owned, features = cold_table.shape
    rows, hidden = targets.shape[0], w_self.shape[1]
    bf16, f32, i32 = jnp.bfloat16, jnp.float32, jnp.int32
    chunked = pltpu.VMEM((PIECES, ngroup, features // PIECES), bf16)
    dma = pltpu.SemaphoreType.DMA
    return pl.pallas_call(
        functools.partial(layer_kernel, nz, nyc, nm),
        out_shape=pltpu.VMEM((rows, hidden), bf16),
        in_specs=[pl.BlockSpec(memory_space=pltpu.HBM)] * len(args),
        out_specs=pl.BlockSpec(memory_space=pltpu.VMEM),
        scratch_shapes=[pltpu.VMEM(a.shape, a.dtype) for a in args]
        + [
            pltpu.VMEM((nyc, 1, LANES), i32),
            pltpu.VMEM((nm, 1, LANES), i32),
            pltpu.VMEM((nyc, 1, LANES), i32),
            pltpu.VMEM((nz, 1, LANES), i32),
            pltpu.VMEM((nz, 1, LANES), i32),
            pltpu.VMEM((nm, 1, LANES), i32),
            pltpu.VMEM((LANES, LANES), i32),
            pltpu.VMEM((ngroup, owned), bf16),
            pltpu.VMEM((ngroup, owned), bf16),
            chunked,
            chunked,
            chunked,
            chunked,
            pltpu.VMEM((ngroup, features), bf16),
            pltpu.VMEM((ngroup // 2, features), bf16),
            pltpu.VMEM((ngroup // 2, features), bf16),
            pltpu.VMEM((ngroup // 2, features), bf16),
            pltpu.VMEM((nz, 1, features), f32),
            pltpu.VMEM((nz, 1, features), f32),
            pltpu.VMEM((nz, features), f32),
            pltpu.VMEM((nm * slots, features), bf16),
            pltpu.VMEM((nm * slots, features), bf16),
            pltpu.VMEM((nm * slots + owner.shape[-1], rows), f32),
            pltpu.VMEM((rows, features), f32),
            pltpu.VMEM((rows, hidden), f32),
            dma((len(args),)),
            dma((3,)),
            dma((3,)),
            dma((nz,)),
            dma((PIECES,)),
            dma((PIECES,)),
            dma((PIECES,)),
            dma((PIECES,)),
            dma((3,)),
            dma((3,)),
            dma,
            dma,
        ],
        compiler_params=pltpu.CompilerParams(
            collective_id=0, has_side_effects=True, vmem_limit_bytes=60 * 1024 * 1024
        ),
        cost_estimate=pl.CostEstimate(
            flops=4 * rows * features * hidden, bytes_accessed=8 * 1024 * 1024, transcendentals=rows
        ),
    )(*args)


def solution(mesh, nyc=16):
    nz = mesh.shape["group"] // nyc
    return jax.shard_map(
        functools.partial(per_device, nz, nyc),
        mesh=mesh,
        in_specs=(
            P(("group", "member"), None),
            P(("group", "member"), None),
            P("member", None),
            P("group", "member", None, None),
            P("group", "member", None),
            P("group", None),
            P("group", "member", None),
            P("group", "member", None),
            P(),
            P(),
            P(),
        ),
        out_specs=P(("group", "member"), None),
        check_vma=False,
    )
```

```python
import functools

import jax
import jax.numpy as jnp
from jax import lax
from jax.experimental import pallas as pl
from jax.experimental.pallas import tpu as pltpu
from jax.sharding import PartitionSpec as P

FANOUT = 25
LANES = 128
PIECES = 6
Z_FIRST = ((0, 2), (2, 1))
Y_FIRST = ((3, 1), (4, 1), (5, 1))
MESH = pl.DeviceIdType.MESH


def wait_bytes(ref, sem):
    pltpu.make_async_copy(ref, ref, sem).wait()


def one_hot(index, width):
    columns = lax.broadcasted_iota(jnp.int32, (index.shape[0], width), 1)
    return (columns == index).astype(jnp.float32).astype(jnp.bfloat16)


def lane_to_rows(row, rows, first):
    wide = jnp.broadcast_to(row, (rows, LANES))
    lane = lax.broadcasted_iota(jnp.int32, (rows, LANES), 1)
    slot = lax.broadcasted_iota(jnp.int32, (rows, LANES), 0)
    return jnp.sum(jnp.where(lane == slot + first, wide, 0), axis=1, keepdims=True)


def exact_dot(a, b):
    return jnp.dot(a, b, preferred_element_type=jnp.float32)


def count_dot(counts, values):
    return lax.dot_general(counts, values, (((0,), (0,)), ((), ())), preferred_element_type=jnp.float32)


def layer_kernel(
    nz,
    nyc,
    nm,
    targets_hbm,
    near_hbm,
    hot_hbm,
    hot_req_hbm,
    live_hbm,
    table_hbm,
    owner_hbm,
    wanted_hbm,
    w_self_hbm,
    w_neigh_hbm,
    bias_hbm,
    out_ref,
    targets_ref,
    near_ref,
    hot_ref,
    hot_req_ref,
    live_ref,
    table_ref,
    owner_ref,
    wanted_ref,
    w_self_ref,
    w_neigh_ref,
    bias_ref,
    ask,
    hot_ask,
    ids_a,
    ids_b,
    ids_c,
    hot_ids,
    square,
    hits,
    hits_x,
    z_out,
    z_in,
    y_out,
    y_in,
    x_out,
    x_core,
    x_send,
    x_in,
    row_out,
    row_in,
    extra,
    h_out,
    h_in,
    tally,
    summed,
    total,
    load_sem,
    send_ids,
    recv_ids,
    recv_ids_z,
    send_z,
    recv_z,
    send_y,
    recv_y,
    send_x,
    recv_x,
    send_h,
    recv_h,
):
    group, member = lax.axis_index("group"), lax.axis_index("member")
    z, yc = group // nyc, group % nyc
    y, core, ny = yc // 2, yc % 2, nyc // 2
    ngroup = nz * nyc
    half = ny * nz
    owned, features = table_ref.shape
    width = features // PIECES
    slots = h_out.shape[0] // nm
    hot_slots = nm * slots
    rows = targets_ref.shape[0]
    bf16, f32, i32 = jnp.bfloat16, jnp.float32, jnp.int32

    def iota(shape, dim):
        return lax.broadcasted_iota(i32, shape, dim)

    def z_peer(step):
        far = nz // 2 - (step + 1) // 2
        return (z + nz + (1 - 2 * (step % 2)) * far) % nz

    def y_peer(step):
        far = ny // 2 - (step + 1) // 2
        return (y + ny + (1 - 2 * (step % 2)) * far) % ny

    def yc_peer(step):
        return y_peer(step // 2) * 2 + (core + 1 + step) % 2

    def m_peer(step):
        return (member + 1 + step) % nm

    def to_z(peer):
        return (peer * nyc + yc, member)

    def to_yc(peer):
        return (z * nyc + peer, member)

    def to_m(peer):
        return (group, peer)

    def each(count, body):
        lax.fori_loop(0, count, lambda i, c: (body(i), c)[1], 0)

    def send(source, target, send_sem, recv_sem, device):
        pltpu.make_async_remote_copy(
            src_ref=source, dst_ref=target, send_sem=send_sem, recv_sem=recv_sem, device_id=device, device_id_type=MESH
        ).start()

    def block(peer, count):
        return pl.ds(pl.multiple_of(peer * count, count), count)

    loads = [
        pltpu.make_async_copy(source, target, load_sem.at[number])
        for number, (source, target) in enumerate(
            [
                (owner_hbm, owner_ref),
                (wanted_hbm, wanted_ref),
                (hot_req_hbm, hot_req_ref),
                (live_hbm, live_ref),
                (bias_hbm, bias_ref),
                (hot_hbm, hot_ref),
                (table_hbm, table_ref),
                (near_hbm, near_ref),
                (targets_hbm, targets_ref),
                (w_self_hbm, w_self_ref),
                (w_neigh_hbm, w_neigh_ref),
            ]
        )
    ]
    for load in loads:
        load.start()

    barrier = pltpu.get_barrier_semaphore()

    def greet(device):
        pl.semaphore_signal(barrier, inc=1, device_id=device, device_id_type=MESH)

    each(nz - 1, lambda i: greet(to_z(z_peer(i))))
    each(nyc - 1, lambda i: greet(to_yc(yc_peer(i))))
    each(nm - 1, lambda i: greet(to_m(m_peer(i))))

    for load in loads[:3]:
        load.wait()
    requests = owner_ref.shape[-1]
    owners = owner_ref[0]
    coded = iota((1, requests), 1) * owned + wanted_ref[0]
    asked = jnp.broadcast_to(owners, (ngroup, requests)) == iota((ngroup, requests), 0)
    coded = jnp.broadcast_to(coded, (ngroup, requests))
    first = jnp.min(jnp.where(asked, coded, requests * owned), axis=1, keepdims=True)
    last = jnp.max(jnp.where(asked, coded, -1), axis=1, keepdims=True)
    twice = last > first
    first_row = jnp.where(first < requests * owned, lax.rem(first, owned), 0)
    last_row = jnp.where(twice, lax.rem(last, owned), -1)
    lane = iota((nyc, LANES), 1)
    packed = jnp.zeros((nyc, LANES), i32)
    for peer in range(nz):
        part = slice(peer * nyc, (peer + 1) * nyc)
        packed = jnp.where(lane == peer, first_row[part], packed)
        packed = jnp.where(lane == nz + peer, last_row[part], packed)
    for peer in range(nyc):
        ask[peer] = packed[peer : peer + 1]
    for peer in range(nm):
        hot_ask[peer] = jnp.zeros((1, LANES), i32)
        hot_ask[peer, :, 0:slots] = hot_req_ref[0, 0, peer : peer + 1, :]

    pl.semaphore_wait(barrier, nz + nyc + nm - 3)

    def send_ids_yc(i):
        peer = yc_peer(i)
        send(ask.at[peer], ids_a.at[yc], send_ids.at[0], recv_ids.at[0], to_yc(peer))

    each(nyc - 1, send_ids_yc)

    def send_ids_m(i):
        peer = m_peer(i)
        send(hot_ask.at[peer], hot_ids.at[member], send_ids.at[2], recv_ids.at[2], to_m(peer))

    each(nm - 1, send_ids_m)
    ids_a[yc] = ask[yc]
    hot_ids[member] = hot_ask[member]
    square[...] = jnp.zeros_like(square)

    loads[7].wait()
    loads[3].wait()
    for first_slot in range(0, tally.shape[0], LANES):
        span = min(LANES, tally.shape[0] - first_slot)
        numbers = iota((span, rows), 0) + first_slot
        counted = jnp.zeros((span, rows), f32)
        for j in range(near_ref.shape[0]):
            counted = counted + jnp.where(near_ref[j : j + 1, :] == numbers, 1.0, 0.0)
        tally[first_slot : first_slot + span, :] = counted
    slot = iota((hot_slots, 1), 0)
    limit = jnp.zeros((hot_slots, 1), i32)
    for peer in range(nm):
        limit = jnp.where(lax.div(slot, slots) == peer, live_ref[0, :, peer : peer + 1], limit)
    hot_tally = jnp.where(lax.rem(slot, slots) < limit, tally[0:hot_slots, :], 0.0).astype(bf16)
    cold_tally = tally[hot_slots:, :]

    wait_bytes(ids_a.at[pl.ds(0, nyc - 1)], recv_ids.at[0])
    for peer in range(nyc):
        square[peer : peer + 1, :] = ids_a[peer]
    square[...] = square[...].T
    for peer in range(nz):
        ids_b[peer, :, 0:nyc] = square[peer : peer + 1, 0:nyc]
        ids_b[peer, :, nyc : 2 * nyc] = square[nz + peer : nz + peer + 1, 0:nyc]

    def send_ids_z(i):
        peer = z_peer(i)
        send(ids_b.at[peer], ids_c.at[z], send_ids.at[1], recv_ids_z.at[z], to_z(peer))

    each(nz - 1, send_ids_z)
    ids_c[z] = ids_b[z]

    wait_bytes(hot_ids.at[pl.ds(0, nm - 1)], recv_ids.at[2])
    loads[5].wait()
    for peer in range(nm):
        wanted_rows = one_hot(lane_to_rows(hot_ids[peer], slots, 0), hot_ref.shape[0])
        h_out[peer * slots : (peer + 1) * slots, :] = exact_dot(wanted_rows, hot_ref[...]).astype(bf16)

    def send_hot(i):
        peer = m_peer(i)
        send(h_out.at[block(peer, slots)], h_in.at[block(member, slots)], send_h, recv_h, to_m(peer))

    each(nm - 1, send_hot)
    h_in[block(member, slots), :] = h_out[block(member, slots), :]

    rows_to = iota((ngroup, ngroup), 0)
    rows_from = iota((ngroup, ngroup), 1)
    turn = (rows_from == lax.rem(rows_to, nz) * nyc + lax.div(rows_to, nz)).astype(f32).astype(bf16)
    turn_back = (rows_from == lax.rem(rows_to, nyc) * nz + lax.div(rows_to, nyc)).astype(f32).astype(bf16)

    loads[6].wait()
    def features_of(chunk):
        return slice(chunk[0] * width, (chunk[0] + chunk[1]) * width)

    def pieces_of(chunk):
        return pl.ds(chunk[0], chunk[1])

    def keep(ref, chunk, rows_of, values):
        for piece in range(chunk[1]):
            ref[chunk[0] + piece, rows_of, :] = values[:, piece * width : (piece + 1) * width].astype(bf16)

    def whole(ref, chunk):
        return jnp.concatenate([ref[chunk[0] + piece] for piece in range(chunk[1])], axis=1)

    offsets = [0]
    for far in range(1, nz // 2):
        offsets += [far, -far]
    offsets += [nz // 2]
    peers = [lax.rem(z + (nz + offset), nz) for offset in offsets]

    def send_batch(chunk, begin, end):
        for number in range(begin, end):
            held = pl.ds(number * nyc, nyc)
            if offsets[number]:
                send(
                    z_out.at[pieces_of(chunk), held],
                    z_in.at[pieces_of(chunk), block(z, nyc)],
                    send_z.at[chunk[0]],
                    recv_z.at[chunk[0]],
                    to_z(peers[number]),
                )
            else:
                z_in[pieces_of(chunk), block(z, nyc), :] = z_out[pieces_of(chunk), held, :]

    early = sum(count for _, count in Z_FIRST)
    cuts = [cut for cut in (0, 5, 9, 13) if cut < nz] + [nz]
    batches = list(zip(cuts[:-1], cuts[1:]))
    for begin, end in batches:
        wanted_rows = []
        for number in range(begin, end):
            peer = peers[number]
            if offsets[number]:
                wait_bytes(ids_c.at[peer], recv_ids_z.at[peer])
            row = ids_c[peer]
            wanted_rows.append(one_hot(lane_to_rows(row, nyc, 0), owned))
            hits[block(peer, nyc), :] = wanted_rows[-1]
            hits_x[block(peer, nyc), :] = one_hot(lane_to_rows(row, nyc, nyc), owned)
        found = exact_dot(jnp.concatenate(wanted_rows, axis=0), table_ref[:, 0 : early * width])
        keep(z_out, (0, early), slice(begin * nyc, end * nyc), found)
        send_batch(Z_FIRST[0], begin, end)
        if begin == 0:
            for chunk in Z_FIRST[1:]:
                send_batch(chunk, begin, end)

    def rows_along_z(chunk, rows_out):
        keep(z_out, chunk, slice(0, ngroup), rows_out)

        def send_rows(i):
            peer = z_peer(i)
            send(
                z_out.at[pieces_of(chunk), block(peer, nyc)],
                z_in.at[pieces_of(chunk), block(z, nyc)],
                send_z.at[chunk[0]],
                recv_z.at[chunk[0]],
                to_z(peer),
            )

        each(nz - 1, send_rows)
        z_in[pieces_of(chunk), block(z, nyc), :] = z_out[pieces_of(chunk), block(z, nyc), :]

    def rows_along_y(chunk, rows_out):
        keep(y_out, chunk, slice(0, ngroup), rows_out)

        def send_rows(i):
            peer = yc_peer(i)
            send(
                y_out.at[pieces_of(chunk), block(peer, nz)],
                y_in.at[pieces_of(chunk), block(yc, nz)],
                send_y.at[chunk[0]],
                recv_y.at[chunk[0]],
                to_yc(peer),
            )

        each(nyc - 1, send_rows)
        y_in[pieces_of(chunk), block(yc, nz), :] = y_out[pieces_of(chunk), block(yc, nz), :]

    def wait_z(chunk, sem=None):
        sem = recv_z if sem is None else sem
        wait_bytes(z_in.at[pieces_of(chunk), pl.ds(0, (nz - 1) * nyc)], sem.at[chunk[0]])

    def wait_y(chunk, sem=None):
        sem = recv_y if sem is None else sem
        wait_bytes(y_in.at[pieces_of(chunk), pl.ds(0, (nyc - 1) * nz)], sem.at[chunk[0]])

    turned = exact_dot(turn, hits[...]).astype(bf16)
    rows_along_y(Y_FIRST[0], exact_dot(turned, table_ref[:, features_of(Y_FIRST[0])]))
    for begin, end in batches[:0:-1]:
        for chunk in Z_FIRST[1:]:
            send_batch(chunk, begin, end)
    for chunk in Y_FIRST[1:]:
        rows_along_y(chunk, exact_dot(turned, table_ref[:, features_of(chunk)]))

    spread = (rows_from == lax.rem(rows_to, nz) * nyc + lax.rem(lax.div(rows_to, nz), ny) * 2 + lax.div(rows_to, half))
    spread = spread.astype(f32).astype(bf16)
    turned = exact_dot(spread, hits_x[...]).astype(bf16)
    x_out[...] = exact_dot(turned, table_ref[...]).astype(bf16)
    send(x_out.at[block(1 - core, half)], x_core, send_x.at[0], recv_x.at[0], to_yc(y * 2 + 1 - core))

    position = iota((ngroup, requests), 1)
    place = (position == lax.div(first, owned)).astype(f32).astype(bf16)
    placed = exact_dot(place, cold_tally.astype(bf16)).astype(bf16)
    placed_turned = exact_dot(turn, placed).astype(bf16)
    last_at = jnp.max(jnp.where(twice, lax.div(last, owned), -1), axis=0, keepdims=True)
    second = jnp.sum(jnp.where(iota((requests, 1), 0) == last_at, cold_tally, 0.0), axis=0, keepdims=True)
    second = jnp.broadcast_to(second, (nz, rows)).astype(bf16)

    wait_bytes(x_core, recv_x.at[0])
    x_send[...] = x_out[block(core, half), :] + x_core[...]

    def send_extra(i):
        peer = y_peer(i)
        send(x_send.at[block(peer, nz)], x_in.at[block(y, nz)], send_x.at[1], recv_x.at[1], to_yc(peer * 2 + core))

    each(ny - 1, send_extra)
    x_in[block(y, nz), :] = x_send[block(y, nz), :]

    for load in loads[8:10]:
        load.wait()
    loads[4].wait()
    total[...] = exact_dot(targets_ref[...], w_self_ref[...]) + bias_ref[...].reshape(1, -1)

    wait_y(Y_FIRST[0])
    rows_along_z(Y_FIRST[0], exact_dot(turn_back, whole(y_in, Y_FIRST[0])))
    wait_z(Z_FIRST[0])
    rows_along_y(Z_FIRST[0], exact_dot(turn, whole(z_in, Z_FIRST[0])))
    for chunk in Y_FIRST[1:]:
        wait_y(chunk)
        rows_along_z(chunk, exact_dot(turn_back, whole(y_in, chunk)))
    for chunk in Z_FIRST[1:]:
        wait_z(chunk)
        rows_along_y(chunk, exact_dot(turn, whole(z_in, chunk)))

    wait_bytes(x_in.at[pl.ds(0, (ny - 1) * nz)], recv_x.at[1])
    target = iota((nz, half), 0)
    source = iota((nz, half), 1)
    pick = (lax.rem(source, nz) == target).astype(f32).astype(bf16)
    picked = exact_dot(pick, x_in[...])
    for peer in range(nz):
        row_out[peer] = picked[peer : peer + 1, :]

    def send_extra_row(i):
        peer = z_peer(i)
        send(row_out.at[peer], row_in.at[z], send_x.at[2], recv_x.at[2], to_z(peer))

    each(nz - 1, send_extra_row)
    row_in[z] = row_out[z]

    wait_bytes(h_in.at[pl.ds(0, (nm - 1) * slots)], recv_h)
    summed[...] = count_dot(hot_tally, h_in[...])

    loads[10].wait()

    def add_chunk(chunk, counts, rows_in):
        part = features_of(chunk)
        aggregate = summed[:, part] + count_dot(counts, rows_in)
        aggregate = (aggregate * (1.0 / FANOUT)).astype(bf16)
        total[...] = total[...] + exact_dot(aggregate, w_neigh_ref[part, :])

    wait_bytes(row_in.at[pl.ds(0, nz - 1)], recv_x.at[2])
    for peer in range(nz):
        extra[peer : peer + 1, :] = row_in[peer]
    summed[...] = summed[...] + count_dot(second, extra[...].astype(bf16))
    wait_y(Z_FIRST[0])
    add_chunk(Z_FIRST[0], placed_turned, whole(y_in, Z_FIRST[0]))
    wait_z(Y_FIRST[0])
    add_chunk(Y_FIRST[0], placed, whole(z_in, Y_FIRST[0]))
    for chunk in Z_FIRST[1:]:
        wait_y(chunk)
        add_chunk(chunk, placed_turned, whole(y_in, chunk))
    for chunk in Y_FIRST[1:]:
        wait_z(chunk)
        add_chunk(chunk, placed, whole(z_in, chunk))
    active = jnp.maximum(total[...], 0.0)
    scale = lax.rsqrt(jnp.mean(active * active, axis=-1, keepdims=True) + 1e-06)
    out_ref[...] = (active * scale).astype(bf16)

    wait_bytes(ids_a.at[pl.ds(0, nyc - 1)], send_ids.at[0])
    wait_bytes(ids_c.at[pl.ds(0, nz - 1)], send_ids.at[1])
    wait_bytes(hot_ids.at[pl.ds(0, nm - 1)], send_ids.at[2])
    wait_bytes(h_in.at[pl.ds(0, (nm - 1) * slots)], send_h)
    wait_bytes(x_core, send_x.at[0])
    wait_bytes(x_in.at[pl.ds(0, (ny - 1) * nz)], send_x.at[1])
    wait_bytes(row_in.at[pl.ds(0, nz - 1)], send_x.at[2])
    for chunk in Z_FIRST + Y_FIRST:
        wait_z(chunk, send_z)
        wait_y(chunk, send_y)


def per_device(nz, nyc, *args):
    targets, near, hot_table, hot_req, live, cold_table, owner, wanted, w_self, w_neigh, bias = args
    args = (targets, near.T) + args[2:]
    nm, slots = hot_req.shape[2:]
    ngroup = nz * nyc
    owned, features = cold_table.shape
    rows, hidden = targets.shape[0], w_self.shape[1]
    bf16, f32, i32 = jnp.bfloat16, jnp.float32, jnp.int32
    chunked = pltpu.VMEM((PIECES, ngroup, features // PIECES), bf16)
    dma = pltpu.SemaphoreType.DMA
    return pl.pallas_call(
        functools.partial(layer_kernel, nz, nyc, nm),
        out_shape=pltpu.VMEM((rows, hidden), bf16),
        in_specs=[pl.BlockSpec(memory_space=pltpu.HBM)] * len(args),
        out_specs=pl.BlockSpec(memory_space=pltpu.VMEM),
        scratch_shapes=[pltpu.VMEM(a.shape, a.dtype) for a in args]
        + [
            pltpu.VMEM((nyc, 1, LANES), i32),
            pltpu.VMEM((nm, 1, LANES), i32),
            pltpu.VMEM((nyc, 1, LANES), i32),
            pltpu.VMEM((nz, 1, LANES), i32),
            pltpu.VMEM((nz, 1, LANES), i32),
            pltpu.VMEM((nm, 1, LANES), i32),
            pltpu.VMEM((LANES, LANES), i32),
            pltpu.VMEM((ngroup, owned), bf16),
            pltpu.VMEM((ngroup, owned), bf16),
            chunked,
            chunked,
            chunked,
            chunked,
            pltpu.VMEM((ngroup, features), bf16),
            pltpu.VMEM((ngroup // 2, features), bf16),
            pltpu.VMEM((ngroup // 2, features), bf16),
            pltpu.VMEM((ngroup // 2, features), bf16),
            pltpu.VMEM((nz, 1, features), f32),
            pltpu.VMEM((nz, 1, features), f32),
            pltpu.VMEM((nz, features), f32),
            pltpu.VMEM((nm * slots, features), bf16),
            pltpu.VMEM((nm * slots, features), bf16),
            pltpu.VMEM((nm * slots + owner.shape[-1], rows), f32),
            pltpu.VMEM((rows, features), f32),
            pltpu.VMEM((rows, hidden), f32),
            dma((len(args),)),
            dma((3,)),
            dma((3,)),
            dma((nz,)),
            dma((PIECES,)),
            dma((PIECES,)),
            dma((PIECES,)),
            dma((PIECES,)),
            dma((3,)),
            dma((3,)),
            dma,
            dma,
        ],
        compiler_params=pltpu.CompilerParams(
            collective_id=0, has_side_effects=True, vmem_limit_bytes=60 * 1024 * 1024
        ),
        cost_estimate=pl.CostEstimate(
            flops=4 * rows * features * hidden, bytes_accessed=8 * 1024 * 1024, transcendentals=rows
        ),
    )(*args)


def solution(mesh, nyc=16):
    nz = mesh.shape["group"] // nyc
    return jax.shard_map(
        functools.partial(per_device, nz, nyc),
        mesh=mesh,
        in_specs=(
            P(("group", "member"), None),
            P(("group", "member"), None),
            P("member", None),
            P("group", "member", None, None),
            P("group", "member", None),
            P("group", None),
            P("group", "member", None),
            P("group", "member", None),
            P(),
            P(),
            P(),
        ),
        out_specs=P(("group", "member"), None),
        check_vma=False,
    )
```

```python
import functools

import jax
import jax.numpy as jnp
from jax import lax
from jax.experimental import pallas as pl
from jax.experimental.pallas import tpu as pltpu
from jax.sharding import PartitionSpec as P

FANOUT = 25
LANES = 128
PIECES = 6
Z_FIRST = ((0, 2), (2, 1))
Y_FIRST = ((3, 1), (4, 1), (5, 1))
MESH = pl.DeviceIdType.MESH


def wait_bytes(ref, sem):
    pltpu.make_async_copy(ref, ref, sem).wait()


def one_hot(index, width):
    columns = lax.broadcasted_iota(jnp.int32, (index.shape[0], width), 1)
    return (columns == index).astype(jnp.float32).astype(jnp.bfloat16)


def lane_to_rows(row, rows, first):
    wide = jnp.broadcast_to(row, (rows, LANES))
    lane = lax.broadcasted_iota(jnp.int32, (rows, LANES), 1)
    slot = lax.broadcasted_iota(jnp.int32, (rows, LANES), 0)
    return jnp.sum(jnp.where(lane == slot + first, wide, 0), axis=1, keepdims=True)


def exact_dot(a, b):
    return jnp.dot(a, b, preferred_element_type=jnp.float32)


def count_dot(counts, values):
    return lax.dot_general(counts, values, (((0,), (0,)), ((), ())), preferred_element_type=jnp.float32)


def layer_kernel(
    nz,
    nyc,
    nm,
    targets_hbm,
    near_hbm,
    hot_hbm,
    hot_req_hbm,
    live_hbm,
    table_hbm,
    owner_hbm,
    wanted_hbm,
    w_self_hbm,
    w_neigh_hbm,
    bias_hbm,
    out_ref,
    targets_ref,
    near_ref,
    hot_ref,
    hot_req_ref,
    live_ref,
    table_ref,
    owner_ref,
    wanted_ref,
    w_self_ref,
    w_neigh_ref,
    bias_ref,
    ask,
    hot_ask,
    ids_a,
    ids_b,
    ids_c,
    hot_ids,
    square,
    hits,
    hits_x,
    z_out,
    z_in,
    y_out,
    y_in,
    x_out,
    x_core,
    x_send,
    x_in,
    row_out,
    row_in,
    extra,
    h_out,
    h_in,
    tally,
    summed,
    total,
    load_sem,
    send_ids,
    recv_ids,
    recv_ids_z,
    send_z,
    recv_z,
    send_y,
    recv_y,
    send_x,
    recv_x,
    send_h,
    recv_h,
):
    group, member = lax.axis_index("group"), lax.axis_index("member")
    z, yc = group // nyc, group % nyc
    y, core, ny = yc // 2, yc % 2, nyc // 2
    ngroup = nz * nyc
    half = ny * nz
    owned, features = table_ref.shape
    width = features // PIECES
    slots = h_out.shape[0] // nm
    hot_slots = nm * slots
    rows = targets_ref.shape[0]
    bf16, f32, i32 = jnp.bfloat16, jnp.float32, jnp.int32

    def iota(shape, dim):
        return lax.broadcasted_iota(i32, shape, dim)

    def z_peer(step):
        far = nz // 2 - (step + 1) // 2
        return (z + nz + (1 - 2 * (step % 2)) * far) % nz

    def y_peer(step):
        far = ny // 2 - (step + 1) // 2
        return (y + ny + (1 - 2 * (step % 2)) * far) % ny

    def yc_peer(step):
        return y_peer(step // 2) * 2 + (core + 1 + step) % 2

    def m_peer(step):
        return (member + 1 + step) % nm

    def to_z(peer):
        return (peer * nyc + yc, member)

    def to_yc(peer):
        return (z * nyc + peer, member)

    def to_m(peer):
        return (group, peer)

    def each(count, body):
        lax.fori_loop(0, count, lambda i, c: (body(i), c)[1], 0)

    def send(source, target, send_sem, recv_sem, device):
        pltpu.make_async_remote_copy(
            src_ref=source, dst_ref=target, send_sem=send_sem, recv_sem=recv_sem, device_id=device, device_id_type=MESH
        ).start()

    def block(peer, count):
        return pl.ds(pl.multiple_of(peer * count, count), count)

    loads = [
        pltpu.make_async_copy(source, target, load_sem.at[number])
        for number, (source, target) in enumerate(
            [
                (owner_hbm, owner_ref),
                (wanted_hbm, wanted_ref),
                (hot_req_hbm, hot_req_ref),
                (live_hbm, live_ref),
                (bias_hbm, bias_ref),
                (hot_hbm, hot_ref),
                (table_hbm, table_ref),
                (near_hbm, near_ref),
                (targets_hbm, targets_ref),
                (w_self_hbm, w_self_ref),
                (w_neigh_hbm, w_neigh_ref),
            ]
        )
    ]
    for load in loads:
        load.start()

    barrier = pltpu.get_barrier_semaphore()

    def greet(device):
        pl.semaphore_signal(barrier, inc=1, device_id=device, device_id_type=MESH)

    each(nz - 1, lambda i: greet(to_z(z_peer(i))))
    each(nyc - 1, lambda i: greet(to_yc(yc_peer(i))))
    each(nm - 1, lambda i: greet(to_m(m_peer(i))))

    for load in loads[:3]:
        load.wait()
    requests = owner_ref.shape[-1]
    owners = owner_ref[0]
    coded = iota((1, requests), 1) * owned + wanted_ref[0]
    asked = jnp.broadcast_to(owners, (ngroup, requests)) == iota((ngroup, requests), 0)
    coded = jnp.broadcast_to(coded, (ngroup, requests))
    first = jnp.min(jnp.where(asked, coded, requests * owned), axis=1, keepdims=True)
    last = jnp.max(jnp.where(asked, coded, -1), axis=1, keepdims=True)
    twice = last > first
    first_row = jnp.where(first < requests * owned, lax.rem(first, owned), 0)
    last_row = jnp.where(twice, lax.rem(last, owned), -1)
    lane = iota((nyc, LANES), 1)
    packed = jnp.zeros((nyc, LANES), i32)
    for peer in range(nz):
        part = slice(peer * nyc, (peer + 1) * nyc)
        packed = jnp.where(lane == peer, first_row[part], packed)
        packed = jnp.where(lane == nz + peer, last_row[part], packed)
    for peer in range(nyc):
        ask[peer] = packed[peer : peer + 1]
    for peer in range(nm):
        hot_ask[peer] = jnp.zeros((1, LANES), i32)
        hot_ask[peer, :, 0:slots] = hot_req_ref[0, 0, peer : peer + 1, :]

    pl.semaphore_wait(barrier, nz + nyc + nm - 3)

    def send_ids_yc(i):
        peer = yc_peer(i)
        send(ask.at[peer], ids_a.at[yc], send_ids.at[0], recv_ids.at[0], to_yc(peer))

    each(nyc - 1, send_ids_yc)

    def send_ids_m(i):
        peer = m_peer(i)
        send(hot_ask.at[peer], hot_ids.at[member], send_ids.at[2], recv_ids.at[2], to_m(peer))

    each(nm - 1, send_ids_m)
    ids_a[yc] = ask[yc]
    hot_ids[member] = hot_ask[member]
    square[...] = jnp.zeros_like(square)

    loads[7].wait()
    loads[3].wait()
    for first_slot in range(0, tally.shape[0], LANES):
        span = min(LANES, tally.shape[0] - first_slot)
        numbers = iota((span, rows), 0) + first_slot
        counted = jnp.zeros((span, rows), f32)
        for j in range(near_ref.shape[0]):
            counted = counted + jnp.where(near_ref[j : j + 1, :] == numbers, 1.0, 0.0)
        tally[first_slot : first_slot + span, :] = counted
    slot = iota((hot_slots, 1), 0)
    limit = jnp.zeros((hot_slots, 1), i32)
    for peer in range(nm):
        limit = jnp.where(lax.div(slot, slots) == peer, live_ref[0, :, peer : peer + 1], limit)
    hot_tally = jnp.where(lax.rem(slot, slots) < limit, tally[0:hot_slots, :], 0.0).astype(bf16)
    cold_tally = tally[hot_slots:, :]

    wait_bytes(ids_a.at[pl.ds(0, nyc - 1)], recv_ids.at[0])
    for peer in range(nyc):
        square[peer : peer + 1, :] = ids_a[peer]
    square[...] = square[...].T
    for peer in range(nz):
        ids_b[peer, :, 0:nyc] = square[peer : peer + 1, 0:nyc]
        ids_b[peer, :, nyc : 2 * nyc] = square[nz + peer : nz + peer + 1, 0:nyc]

    def send_ids_z(i):
        peer = z_peer(i)
        send(ids_b.at[peer], ids_c.at[z], send_ids.at[1], recv_ids_z.at[z], to_z(peer))

    each(nz - 1, send_ids_z)
    ids_c[z] = ids_b[z]

    wait_bytes(hot_ids.at[pl.ds(0, nm - 1)], recv_ids.at[2])
    loads[5].wait()
    for peer in range(nm):
        wanted_rows = one_hot(lane_to_rows(hot_ids[peer], slots, 0), hot_ref.shape[0])
        h_out[peer * slots : (peer + 1) * slots, :] = exact_dot(wanted_rows, hot_ref[...]).astype(bf16)

    def send_hot(i):
        peer = m_peer(i)
        send(h_out.at[block(peer, slots)], h_in.at[block(member, slots)], send_h, recv_h, to_m(peer))

    each(nm - 1, send_hot)
    h_in[block(member, slots), :] = h_out[block(member, slots), :]

    rows_to = iota((ngroup, ngroup), 0)
    rows_from = iota((ngroup, ngroup), 1)
    turn = (rows_from == lax.rem(rows_to, nz) * nyc + lax.div(rows_to, nz)).astype(f32).astype(bf16)
    turn_back = (rows_from == lax.rem(rows_to, nyc) * nz + lax.div(rows_to, nyc)).astype(f32).astype(bf16)

    loads[6].wait()
    def features_of(chunk):
        return slice(chunk[0] * width, (chunk[0] + chunk[1]) * width)

    def pieces_of(chunk):
        return pl.ds(chunk[0], chunk[1])

    def keep(ref, chunk, rows_of, values):
        for piece in range(chunk[1]):
            ref[chunk[0] + piece, rows_of, :] = values[:, piece * width : (piece + 1) * width].astype(bf16)

    def whole(ref, chunk):
        return jnp.concatenate([ref[chunk[0] + piece] for piece in range(chunk[1])], axis=1)

    offsets = [0]
    for far in range(1, nz // 2):
        offsets += [far, -far]
    offsets += [nz // 2]
    peers = [lax.rem(z + (nz + offset), nz) for offset in offsets]

    def send_batch(chunk, begin, end):
        for number in range(begin, end):
            held = pl.ds(number * nyc, nyc)
            if offsets[number]:
                send(
                    z_out.at[pieces_of(chunk), held],
                    z_in.at[pieces_of(chunk), block(z, nyc)],
                    send_z.at[chunk[0]],
                    recv_z.at[chunk[0]],
                    to_z(peers[number]),
                )
            else:
                z_in[pieces_of(chunk), block(z, nyc), :] = z_out[pieces_of(chunk), held, :]

    early = sum(count for _, count in Z_FIRST)
    cuts = [cut for cut in (0, 5, 9, 13) if cut < nz] + [nz]
    batches = list(zip(cuts[:-1], cuts[1:]))
    for begin, end in batches:
        wanted_rows = []
        for number in range(begin, end):
            peer = peers[number]
            if offsets[number]:
                wait_bytes(ids_c.at[peer], recv_ids_z.at[peer])
            row = ids_c[peer]
            wanted_rows.append(one_hot(lane_to_rows(row, nyc, 0), owned))
            hits[block(peer, nyc), :] = wanted_rows[-1]
            hits_x[block(peer, nyc), :] = one_hot(lane_to_rows(row, nyc, nyc), owned)
        found = exact_dot(jnp.concatenate(wanted_rows, axis=0), table_ref[:, 0 : early * width])
        keep(z_out, (0, early), slice(begin * nyc, end * nyc), found)
        send_batch(Z_FIRST[0], begin, end)
        if begin == 0:
            for chunk in Z_FIRST[1:]:
                send_batch(chunk, begin, end)

    def rows_along_z(chunk, rows_out):
        keep(z_out, chunk, slice(0, ngroup), rows_out)

        def send_rows(i):
            peer = z_peer(i)
            send(
                z_out.at[pieces_of(chunk), block(peer, nyc)],
                z_in.at[pieces_of(chunk), block(z, nyc)],
                send_z.at[chunk[0]],
                recv_z.at[chunk[0]],
                to_z(peer),
            )

        each(nz - 1, send_rows)
        z_in[pieces_of(chunk), block(z, nyc), :] = z_out[pieces_of(chunk), block(z, nyc), :]

    def rows_along_y(chunk, rows_out):
        keep(y_out, chunk, slice(0, ngroup), rows_out)

        def send_rows(i):
            peer = yc_peer(i)
            send(
                y_out.at[pieces_of(chunk), block(peer, nz)],
                y_in.at[pieces_of(chunk), block(yc, nz)],
                send_y.at[chunk[0]],
                recv_y.at[chunk[0]],
                to_yc(peer),
            )

        each(nyc - 1, send_rows)
        y_in[pieces_of(chunk), block(yc, nz), :] = y_out[pieces_of(chunk), block(yc, nz), :]

    def wait_z(chunk, sem=None):
        sem = recv_z if sem is None else sem
        wait_bytes(z_in.at[pieces_of(chunk), pl.ds(0, (nz - 1) * nyc)], sem.at[chunk[0]])

    def wait_y(chunk, sem=None):
        sem = recv_y if sem is None else sem
        wait_bytes(y_in.at[pieces_of(chunk), pl.ds(0, (nyc - 1) * nz)], sem.at[chunk[0]])

    turned = exact_dot(turn, hits[...]).astype(bf16)
    rows_along_y(Y_FIRST[0], exact_dot(turned, table_ref[:, features_of(Y_FIRST[0])]))
    for begin, end in batches[:0:-1]:
        for chunk in Z_FIRST[1:]:
            send_batch(chunk, begin, end)
    for chunk in Y_FIRST[1:]:
        rows_along_y(chunk, exact_dot(turned, table_ref[:, features_of(chunk)]))

    spread = (rows_from == lax.rem(rows_to, nz) * nyc + lax.rem(lax.div(rows_to, nz), ny) * 2 + lax.div(rows_to, half))
    spread = spread.astype(f32).astype(bf16)
    turned = exact_dot(spread, hits_x[...]).astype(bf16)
    x_out[...] = exact_dot(turned, table_ref[...]).astype(bf16)
    send(x_out.at[block(1 - core, half)], x_core, send_x.at[0], recv_x.at[0], to_yc(y * 2 + 1 - core))

    position = iota((ngroup, requests), 1)
    place = (position == lax.div(first, owned)).astype(f32).astype(bf16)
    placed = exact_dot(place, cold_tally.astype(bf16)).astype(bf16)
    placed_turned = exact_dot(turn, placed).astype(bf16)
    last_at = jnp.max(jnp.where(twice, lax.div(last, owned), -1), axis=0, keepdims=True)
    second = jnp.sum(jnp.where(iota((requests, 1), 0) == last_at, cold_tally, 0.0), axis=0, keepdims=True)
    second = jnp.broadcast_to(second, (nz, rows)).astype(bf16)

    wait_bytes(x_core, recv_x.at[0])
    x_send[...] = x_out[block(core, half), :] + x_core[...]

    def send_extra(i):
        peer = y_peer(i)
        send(x_send.at[block(peer, nz)], x_in.at[block(y, nz)], send_x.at[1], recv_x.at[1], to_yc(peer * 2 + core))

    each(ny - 1, send_extra)
    x_in[block(y, nz), :] = x_send[block(y, nz), :]

    for load in loads[8:10]:
        load.wait()
    loads[4].wait()
    total[...] = exact_dot(targets_ref[...], w_self_ref[...]) + bias_ref[...].reshape(1, -1)

    wait_y(Y_FIRST[0])
    rows_along_z(Y_FIRST[0], exact_dot(turn_back, whole(y_in, Y_FIRST[0])))
    wait_z(Z_FIRST[0])
    rows_along_y(Z_FIRST[0], exact_dot(turn, whole(z_in, Z_FIRST[0])))
    for chunk in Y_FIRST[1:]:
        wait_y(chunk)
        rows_along_z(chunk, exact_dot(turn_back, whole(y_in, chunk)))
    for chunk in Z_FIRST[1:]:
        wait_z(chunk)
        rows_along_y(chunk, exact_dot(turn, whole(z_in, chunk)))

    wait_bytes(x_in.at[pl.ds(0, (ny - 1) * nz)], recv_x.at[1])
    target = iota((nz, half), 0)
    source = iota((nz, half), 1)
    pick = (lax.rem(source, nz) == target).astype(f32).astype(bf16)
    picked = exact_dot(pick, x_in[...])
    for peer in range(nz):
        row_out[peer] = picked[peer : peer + 1, :]

    def send_extra_row(i):
        peer = z_peer(i)
        send(row_out.at[peer], row_in.at[z], send_x.at[2], recv_x.at[2], to_z(peer))

    each(nz - 1, send_extra_row)
    row_in[z] = row_out[z]

    wait_bytes(h_in.at[pl.ds(0, (nm - 1) * slots)], recv_h)
    summed[...] = count_dot(hot_tally, h_in[...])

    loads[10].wait()

    def add_chunk(chunk, counts, rows_in):
        part = features_of(chunk)
        summed[:, part] = summed[:, part] + count_dot(counts, rows_in)

    wait_y(Z_FIRST[0])
    add_chunk(Z_FIRST[0], placed_turned, whole(y_in, Z_FIRST[0]))
    wait_z(Y_FIRST[0])
    add_chunk(Y_FIRST[0], placed, whole(z_in, Y_FIRST[0]))
    for chunk in Z_FIRST[1:]:
        wait_y(chunk)
        add_chunk(chunk, placed_turned, whole(y_in, chunk))
    for chunk in Y_FIRST[1:-1]:
        wait_z(chunk)
        add_chunk(chunk, placed, whole(z_in, chunk))
    wait_bytes(row_in.at[pl.ds(0, nz - 1)], recv_x.at[2])
    for peer in range(nz):
        extra[peer : peer + 1, :] = row_in[peer]
    summed[...] = summed[...] + count_dot(second, extra[...].astype(bf16))
    wait_z(Y_FIRST[-1])
    add_chunk(Y_FIRST[-1], placed, whole(z_in, Y_FIRST[-1]))
    tile = rows // 2
    for first_target in range(0, rows, tile):
        part = slice(first_target, first_target + tile)
        aggregate = (summed[part, :] * (1.0 / FANOUT)).astype(bf16)
        active = jnp.maximum(total[part, :] + exact_dot(aggregate, w_neigh_ref[...]), 0.0)
        scale = lax.rsqrt(jnp.mean(active * active, axis=-1, keepdims=True) + 1e-06)
        out_ref[part, :] = (active * scale).astype(bf16)

    wait_bytes(ids_a.at[pl.ds(0, nyc - 1)], send_ids.at[0])
    wait_bytes(ids_c.at[pl.ds(0, nz - 1)], send_ids.at[1])
    wait_bytes(hot_ids.at[pl.ds(0, nm - 1)], send_ids.at[2])
    wait_bytes(h_in.at[pl.ds(0, (nm - 1) * slots)], send_h)
    wait_bytes(x_core, send_x.at[0])
    wait_bytes(x_in.at[pl.ds(0, (ny - 1) * nz)], send_x.at[1])
    wait_bytes(row_in.at[pl.ds(0, nz - 1)], send_x.at[2])
    for chunk in Z_FIRST + Y_FIRST:
        wait_z(chunk, send_z)
        wait_y(chunk, send_y)


def per_device(nz, nyc, *args):
    targets, near, hot_table, hot_req, live, cold_table, owner, wanted, w_self, w_neigh, bias = args
    args = (targets, near.T) + args[2:]
    nm, slots = hot_req.shape[2:]
    ngroup = nz * nyc
    owned, features = cold_table.shape
    rows, hidden = targets.shape[0], w_self.shape[1]
    bf16, f32, i32 = jnp.bfloat16, jnp.float32, jnp.int32
    chunked = pltpu.VMEM((PIECES, ngroup, features // PIECES), bf16)
    dma = pltpu.SemaphoreType.DMA
    return pl.pallas_call(
        functools.partial(layer_kernel, nz, nyc, nm),
        out_shape=pltpu.VMEM((rows, hidden), bf16),
        in_specs=[pl.BlockSpec(memory_space=pltpu.HBM)] * len(args),
        out_specs=pl.BlockSpec(memory_space=pltpu.VMEM),
        scratch_shapes=[pltpu.VMEM(a.shape, a.dtype) for a in args]
        + [
            pltpu.VMEM((nyc, 1, LANES), i32),
            pltpu.VMEM((nm, 1, LANES), i32),
            pltpu.VMEM((nyc, 1, LANES), i32),
            pltpu.VMEM((nz, 1, LANES), i32),
            pltpu.VMEM((nz, 1, LANES), i32),
            pltpu.VMEM((nm, 1, LANES), i32),
            pltpu.VMEM((LANES, LANES), i32),
            pltpu.VMEM((ngroup, owned), bf16),
            pltpu.VMEM((ngroup, owned), bf16),
            chunked,
            chunked,
            chunked,
            chunked,
            pltpu.VMEM((ngroup, features), bf16),
            pltpu.VMEM((ngroup // 2, features), bf16),
            pltpu.VMEM((ngroup // 2, features), bf16),
            pltpu.VMEM((ngroup // 2, features), bf16),
            pltpu.VMEM((nz, 1, features), f32),
            pltpu.VMEM((nz, 1, features), f32),
            pltpu.VMEM((nz, features), f32),
            pltpu.VMEM((nm * slots, features), bf16),
            pltpu.VMEM((nm * slots, features), bf16),
            pltpu.VMEM((nm * slots + owner.shape[-1], rows), f32),
            pltpu.VMEM((rows, features), f32),
            pltpu.VMEM((rows, hidden), f32),
            dma((len(args),)),
            dma((3,)),
            dma((3,)),
            dma((nz,)),
            dma((PIECES,)),
            dma((PIECES,)),
            dma((PIECES,)),
            dma((PIECES,)),
            dma((3,)),
            dma((3,)),
            dma,
            dma,
        ],
        compiler_params=pltpu.CompilerParams(
            collective_id=0, has_side_effects=True, vmem_limit_bytes=60 * 1024 * 1024
        ),
        cost_estimate=pl.CostEstimate(
            flops=4 * rows * features * hidden, bytes_accessed=8 * 1024 * 1024, transcendentals=rows
        ),
    )(*args)


def solution(mesh, nyc=16):
    nz = mesh.shape["group"] // nyc
    return jax.shard_map(
        functools.partial(per_device, nz, nyc),
        mesh=mesh,
        in_specs=(
            P(("group", "member"), None),
            P(("group", "member"), None),
            P("member", None),
            P("group", "member", None, None),
            P("group", "member", None),
            P("group", None),
            P("group", "member", None),
            P("group", "member", None),
            P(),
            P(),
            P(),
        ),
        out_specs=P(("group", "member"), None),
        check_vma=False,
    )
```
